32 devices in a mesh: section: 8 (over y, x, core), expert: 4 (over z).
Axes of the slice: x: 2, y: 2, z: 4, core: 2. Of those that a mesh axis runs over, the one named last changes fastest.
Arguments:
- grad_out: bfloat16 [8, 512, 1024], P('section', 'expert'), may hold values from -6 to 6
- saved_inputs: bfloat16 [8, 2, 512, 1024], P('section', None, 'expert'), may hold values from -6 to 6
- routes: int32 [8, 2, 512, 8], P('section', None, 'expert'), may hold values from 0 to 31, all different within a row; in each aligned block of 128 rows (0 to 127, 128 to 255, ..., all dimensions but the last counted through in order) at most 40 rows name the same one
- gate_weights: float32 [8, 2, 512, 8], P('section', None, 'expert'), may hold values from 0.05 to 0.3
- w_gate: bfloat16 [8, 32, 1024, 512], P('section', 'expert'), may hold values from -0.1875 to 0.1875
- w_up: bfloat16 [8, 32, 1024, 512], P('section', 'expert'), may hold values from -0.1875 to 0.1875
- w_down: bfloat16 [8, 32, 512, 1024], P('section', 'expert'), may hold values from -0.25 to 0.25
Outputs:
- input_grad: bfloat16 [8, 512, 1024], P('section', 'expert')
The draws below stay inside these ranges and needn't reach their ends.
Inputs may be any that keep to these rules, and one draw needn't show every extreme that they name: `routes`: each row names 8 different experts. In the rows of one device at one step (aligned blocks of 128 rows) no expert is named by more than 40 rows; in some blocks one expert is named by exactly 40.
All inputs are finite; a program needn't handle non-finite values.
Results may differ from the reference program's by a relative error of at most 0.007.
Values may be sent and summed in bfloat16 or wider, within the bound.
No kernel may reach another device: no remote copies, remote signals or barrier semaphores. Data moves between devices by JAX's collectives and lax.ppermute only.
A program may use at most 128 MiB of HBM per device.

```python
import math
import jax
import jax.numpy as jnp
import numpy as np
from jax import lax

D = 1024
H = 512
EXPERTS = 32
TOP = 8
TOK_DEV = 128
TICKS = 2
MOST = 40
TOKENS = 512
SECTIONS = 8
N_EXPERT = 4


def level_of(key, shape, pieces, smallest, high):
    def one(dim, blocks):
        heights = jax.random.uniform(jax.random.fold_in(jax.random.fold_in(key, 6), dim), (blocks,), jnp.float32, smallest / len(pieces), high / len(pieces))
        return jnp.repeat(jnp.exp(heights), shape[dim] // blocks).reshape((-1,) + (1,) * (len(shape) - dim - 1))

    loudness = one(*pieces[0])
    for cut in pieces[1:]:
        loudness = loudness * one(*cut)
    return loudness


def assign_block(own_key, own, number, rows, count, top, bound, skew):
    sequence = jax.random.permutation(own_key, count)
    heavy_load, ordinary = portions_of(count, rows * top, bound, skew, True), portions_of(count, rows * top, bound, skew, False)
    places = jnp.arange(count)

    def named(lengths, rotation):
        used = int((lengths > 0).sum())
        fixed = max(1, used // 4)
        moved = fixed + (places - fixed + rotation * (used - fixed)) % max(1, count - fixed)
        return jnp.zeros((count,), jnp.int32).at[sequence[jnp.where(places < fixed, places, moved)]].set(jnp.asarray(lengths, jnp.int32))

    lengths = jnp.where(number % 4 == 0, named(heavy_load, number // 4), named(ordinary, number - number // 4 - 1))
    mixed = jax.random.permutation(jax.random.fold_in(own, 3), count)
    source_of, taker = mixed[0:count // 2 * 2:2], mixed[1:count // 2 * 2:2]
    slack = jnp.minimum(lengths[source_of] - 1, bound - lengths[taker]) // 2
    slack = jnp.where((source_of == sequence[0]) | (taker == sequence[0]) | (lengths[taker] == 0), 0, jnp.maximum(slack, 0))
    moved = jax.random.randint(jax.random.fold_in(own, 4), (count // 2,), 0, 1 << 20) % (slack + 1)
    lengths = lengths.at[source_of].add(-moved).at[taker].add(moved)
    labels = jnp.searchsorted(jnp.cumsum(lengths), jnp.arange(rows * top), side="right").astype(jnp.int32)
    table = labels.reshape(top, rows).T
    table = table[jax.random.permutation(jax.random.fold_in(own, 1), rows)]
    rotation = jax.random.randint(jax.random.fold_in(own, 2), (rows, 1), 0, top)
    return jnp.take_along_axis(table, (jnp.arange(top)[None, :] + rotation) % top, axis=1)


def portions_of(count, total, limit, lean, full):
    portions = [(1 << 20) // math.isqrt(standing ** lean) + 1 for standing in range(1, count + 1)]
    largest = limit if full else min(limit, max(-(-total // count), total * portions[0] // sum(portions)))
    least = 1 if total - largest >= count - 1 else 0
    counts, spare = [largest] + [least] * (count - 1), total - largest - least * (count - 1)
    while spare > 0:
        candidates = [i for i in range(1, count) if counts[i] < largest] or [i for i in range(1, count) if counts[i] < limit]
        whole, left = sum([portions[i] for i in candidates]), spare
        for i in candidates:
            addition = min(limit - counts[i], max(1, left * portions[i] // whole), spare)
            counts[i] = counts[i] + addition
            spare = spare - addition
    return np.array(counts)


def scatter_about(own_key, shape, spread, most, cuts=(), kind=jnp.bfloat16):
    level = level_of(own_key, shape, cuts, -0.22, 0.18) if cuts else 1.0
    entries = jax.random.normal(own_key, shape, jnp.float32) * spread * level
    return jnp.minimum(jnp.maximum(entries, -most), most).astype(kind)


def setup_inputs(seed: int = 0) -> dict:
    seeds = jax.random.split(jax.random.key(seed), 8)
    grad_out = scatter_about(seeds[0], (SECTIONS, TOKENS, D), 1.0, 6.0, ((0, 8), (1, 4)))
    saved_inputs = scatter_about(seeds[1], (SECTIONS, TICKS, TOKENS, D), 1.0, 6.0, ((0, 8), (2, 4)))
    routes_keys = jax.random.split(jax.random.fold_in(seeds[2], 1), SECTIONS * TICKS * TOKENS // TOK_DEV)
    routes_turns = jax.random.permutation(jax.random.fold_in(seeds[2], 3), SECTIONS * TICKS * TOKENS // TOK_DEV)
    routes = jax.vmap(lambda own, number: assign_block(jax.random.fold_in(seeds[2], 2), own, number, TOK_DEV, EXPERTS, TOP, MOST, 2))(routes_keys, routes_turns).reshape((SECTIONS, TICKS, TOKENS, TOP))
    gate_weights = jnp.clip(0.05 + 0.25 * jax.random.uniform(seeds[3], (SECTIONS, TICKS, TOKENS, TOP), jnp.float32) ** level_of(seeds[3], (SECTIONS, TICKS, TOKENS, TOP), ((0, 8), (2, 4)), -0.2, 0.2), 0.05, 0.3)
    w_gate = scatter_about(seeds[4], (SECTIONS, EXPERTS, D, H), D ** -0.5, 0.1875, ((0, 8), (1, 4)))
    w_up = scatter_about(seeds[5], (SECTIONS, EXPERTS, D, H), D ** -0.5, 0.1875, ((0, 8), (1, 4)))
    w_down = scatter_about(seeds[6], (SECTIONS, EXPERTS, H, D), H ** -0.5, 0.25, ((0, 8), (1, 4)))
    return dict(grad_out=grad_out, saved_inputs=saved_inputs, routes=routes, gate_weights=gate_weights, w_gate=w_gate, w_up=w_up, w_down=w_down)


def expert_rows(input_rows, grad_rows, gate_proj, up_proj, down_proj):
    inputs_f = input_rows.astype(jnp.float32)
    gate_pre = jnp.einsum("emd,edh->emh", inputs_f, gate_proj.astype(jnp.float32))
    up_pre = jnp.einsum("emd,edh->emh", inputs_f, up_proj.astype(jnp.float32))
    hidden_grad = jnp.einsum("emd,ehd->emh", grad_rows.astype(jnp.float32), down_proj.astype(jnp.float32))
    sigmoid_gate = jax.nn.sigmoid(gate_pre)
    gate_grad = (hidden_grad * up_pre * sigmoid_gate * (1.0 + gate_pre * (1.0 - sigmoid_gate))).astype(jnp.bfloat16)
    up_grad = (hidden_grad * gate_pre * sigmoid_gate).astype(jnp.bfloat16)
    row_grad = jnp.einsum("emh,edh->emd", gate_grad.astype(jnp.float32), gate_proj.astype(jnp.float32))
    row_grad = row_grad + jnp.einsum("emh,edh->emd", up_grad.astype(jnp.float32), up_proj.astype(jnp.float32))
    return row_grad.astype(jnp.bfloat16)


def section_step(operands):
    grad, saved, route_ids, weights, gate_proj, up_proj, down_proj = operands
    row_total = TOKENS * TOP
    flat_routes = route_ids.reshape(-1).astype(jnp.int32)
    one_hot = (flat_routes[:, None] == jnp.arange(EXPERTS, dtype=jnp.int32)[None, :]).astype(jnp.int32)
    blocks = one_hot.reshape(N_EXPERT, TOK_DEV * TOP, EXPERTS)
    earlier = jnp.cumsum(blocks, axis=1) - blocks
    position = jnp.sum(earlier * blocks, axis=2).reshape(-1)
    owner_rank = jnp.arange(row_total, dtype=jnp.int32) // (TOK_DEV * TOP)
    capacity = N_EXPERT * MOST
    slot_index = flat_routes * capacity + owner_rank * MOST + position
    token_index = jnp.arange(row_total, dtype=jnp.int32) // TOP
    slot_token = jnp.zeros((EXPERTS * capacity,), jnp.int32).at[slot_index].set(token_index)
    slot_live = jnp.zeros((EXPERTS * capacity,), jnp.int32).at[slot_index].set(1)
    input_rows = jnp.where(slot_live[:, None] == 1, saved[slot_token], jnp.zeros((), saved.dtype))
    grad_rows = jnp.where(slot_live[:, None] == 1, grad[slot_token], jnp.zeros((), grad.dtype))
    row_grad = expert_rows(input_rows.reshape(EXPERTS, capacity, D), grad_rows.reshape(EXPERTS, capacity, D), gate_proj, up_proj, down_proj)
    back_rows = row_grad.reshape(EXPERTS * capacity, D)[slot_index].reshape(TOKENS, TOP, D)
    total = grad.astype(jnp.float32) + jnp.sum(weights[:, :, None].astype(jnp.float32) * back_rows.astype(jnp.float32), axis=1)
    return total.astype(jnp.bfloat16)


def reference(grad_out, saved_inputs, routes, gate_weights, w_gate, w_up, w_down):
    grad = grad_out
    result = grad_out
    for step_index in range(TICKS):
        result = lax.map(section_step, (grad, saved_inputs[:, step_index], routes[:, step_index], gate_weights[:, step_index], w_gate, w_up, w_down))
        if step_index + 1 < TICKS:
            grad = jnp.roll(result, -1, axis=0)
    return result
```

```python
import functools

import jax
import jax.numpy as jnp
from jax import lax
from jax.experimental import pallas as pl
from jax.experimental.pallas import tpu as pltpu
from jax.sharding import PartitionSpec as P

MOST = 40
PAIR = 2 * MOST
F32 = jnp.float32
BF16 = jnp.bfloat16


def dot(a, b, dims):
    return lax.dot_general(a, b, (dims, ((), ())), preferred_element_type=F32)


def expanded(local):
    slot = lax.broadcasted_iota(jnp.int32, (local, local * PAIR), 1)
    first = lax.broadcasted_iota(jnp.int32, (local, local * PAIR), 0) * PAIR
    return jnp.where((slot >= first) & (slot < first + PAIR), 1.0, 0.0).astype(BF16)


def forward_kernel(sources, local, step, base_ref, *refs):
    x_refs, refs = refs[:sources], refs[sources:]
    meta_refs, refs = refs[:sources], refs[sources:]
    gate_ref, up_ref, a_ref, b_ref, pick_ref, place_ref, rows_ref, weight_ref = refs
    tokens = x_refs[0].shape[0]
    width = x_refs[0].shape[1]
    top = meta_refs[0].shape[1] // 2

    @pl.when(pl.program_id(0) == 0)
    def _():
        mine = lax.broadcasted_iota(jnp.int32, (local, tokens), 0).astype(F32) + base_ref[0].astype(F32)
        before = (
            lax.broadcasted_iota(jnp.int32, (tokens, tokens), 0)
            < lax.broadcasted_iota(jnp.int32, (tokens, tokens), 1)
        )
        before = jnp.where(before, 1.0, 0.0).astype(BF16)
        table = expanded(local)
        for pair in range(sources // 2):
            targets, weights = [], []
            for half in range(2):
                meta = meta_refs[2 * pair + half][step]
                named = jnp.zeros((local, tokens), F32)
                weight = jnp.zeros((local, tokens), F32)
                for k in range(top):
                    same = meta[k : k + 1] == mine
                    named = jnp.where(same, 1.0, named)
                    weight = jnp.where(same, meta[top + k : top + k + 1], weight)
                position = dot(named.astype(BF16), before, ((1,), (0,)))
                targets.append(jnp.where(named > 0.5, position + half * MOST, -1.0))
                weights.append(weight)
            target = jnp.concatenate(targets, axis=1).astype(BF16)
            weight = jnp.concatenate(weights, axis=1)
            spread = dot(table, target, ((0,), (0,)))
            slot = lax.broadcasted_iota(jnp.int32, spread.shape, 0) % PAIR
            picked = spread == slot.astype(F32)
            pick = jnp.where(picked, 1.0, 0.0)
            pick_ref[pair] = pick.astype(BF16)
            spread_t = dot(target, table, ((0,), (0,)))
            slot_t = lax.broadcasted_iota(jnp.int32, spread_t.shape, 1) % PAIR
            place_ref[pair] = jnp.where(spread_t == slot_t.astype(F32), 1.0, 0.0).astype(BF16)
            for e in range(local):
                block = jnp.where(picked[e * PAIR : (e + 1) * PAIR], weight[e : e + 1], 0.0)
                weight_ref[e, pair * PAIR : (pair + 1) * PAIR, :] = jnp.sum(block, axis=1, keepdims=True)
            source = jnp.concatenate([x_refs[2 * pair][...], x_refs[2 * pair + 1][...]], axis=0)
            for n in range(0, width, 256):
                rows = dot(pick_ref[pair], source[:, n : n + 256], ((1,), (0,))).astype(BF16)
                rows_ref[:, pair * PAIR : (pair + 1) * PAIR, n : n + 256] = rows.reshape(local, PAIR, 256)

    e = pl.program_id(0)
    rows = rows_ref[e]
    gate = dot(rows, gate_ref[0], ((1,), (0,)))
    up = dot(rows, up_ref[0], ((1,), (0,)))
    sig = 1.0 / (1.0 + jnp.exp(-gate))
    scaled = sig * weight_ref[e]
    a_ref[0] = up * scaled * (1.0 + gate * (1.0 - sig))
    b_ref[0] = gate * scaled


def backward_kernel(sources, local, *refs):
    g_refs, refs = refs[:sources], refs[sources:]
    a_ref, b_ref, pick_ref, place_ref, gate_ref, up_ref, down_ref = refs[:7]
    out_refs, refs = refs[7 : 7 + sources], refs[7 + sources :]
    rows_ref, back_ref = refs
    tokens, width = g_refs[0].shape
    e = pl.program_id(0)

    @pl.when(e == 0)
    def _():
        for pair in range(sources // 2):
            source = jnp.concatenate([g_refs[2 * pair][...], g_refs[2 * pair + 1][...]], axis=0)
            for n in range(0, width, 256):
                rows = dot(pick_ref[pair], source[:, n : n + 256], ((1,), (0,))).astype(BF16)
                rows_ref[:, pair * PAIR : (pair + 1) * PAIR, n : n + 256] = rows.reshape(local, PAIR, 256)

    hidden = dot(rows_ref[e], down_ref[0], ((1,), (1,)))
    gate_grad = (hidden * a_ref[0]).astype(BF16)
    up_grad = (hidden * b_ref[0]).astype(BF16)
    row = dot(gate_grad, gate_ref[0], ((1,), (1,))) + dot(up_grad, up_ref[0], ((1,), (1,)))
    row = row.astype(BF16)
    for pair in range(sources // 2):
        back_ref[pair, e] = row[pair * PAIR : (pair + 1) * PAIR]

    @pl.when(e == local - 1)
    def _():
        for pair in range(sources // 2):
            for n in range(0, width, 256):
                rows = back_ref[pair, :, :, n : n + 256].reshape(local * PAIR, 256)
                total = dot(place_ref[pair], rows, ((1,), (0,)))
                for half in range(2):
                    out = out_refs[2 * pair + half]
                    out[:, n : n + 256] = total[half * tokens : (half + 1) * tokens].astype(out.dtype)


def whole(shape):
    return pl.BlockSpec(shape, lambda e: (0,) * len(shape))


def one(shape):
    return pl.BlockSpec((1,) + shape[1:], lambda e: (e,) + (0,) * (len(shape) - 1))


def forward(step, base, xs, metas, gate, up):
    sources, local = len(xs), gate.shape[0]
    tokens, width = xs[0].shape
    hidden = gate.shape[2]
    rows = sources * MOST
    factor = jax.ShapeDtypeStruct((local, rows, hidden), F32)
    pick = jax.ShapeDtypeStruct((sources // 2, local * PAIR, 2 * tokens), BF16)
    place = jax.ShapeDtypeStruct((sources // 2, 2 * tokens, local * PAIR), BF16)
    outs = (factor, factor, pick, place)
    return pl.pallas_call(
        functools.partial(forward_kernel, sources, local, step),
        grid=(local,),
        in_specs=[pl.BlockSpec(memory_space=pltpu.SMEM)]
        + [whole(x.shape) for x in xs]
        + [whole(m.shape) for m in metas]
        + [one(gate.shape), one(up.shape)],
        out_specs=(one(factor.shape), one(factor.shape), whole(pick.shape), whole(place.shape)),
        out_shape=outs,
        scratch_shapes=[
            pltpu.VMEM((local, rows, width), BF16),
            pltpu.VMEM((local, rows, 1), F32),
        ],
        compiler_params=pltpu.CompilerParams(vmem_limit_bytes=32 * 1024 * 1024),
        cost_estimate=pl.CostEstimate(
            flops=4 * local * rows * width * hidden,
            bytes_accessed=4 * local * width * hidden,
            transcendentals=local * rows * hidden,
        ),
        name="forward",
    )(base, *xs, *metas, gate, up)


def backward(gs, a, b, pick, place, gate, up, down):
    sources, local = len(gs), gate.shape[0]
    tokens, width = gs[0].shape
    hidden = gate.shape[2]
    rows = sources * MOST
    outs = tuple(
        jax.ShapeDtypeStruct((tokens, width), F32 if k == 0 else BF16) for k in range(sources)
    )
    return pl.pallas_call(
        functools.partial(backward_kernel, sources, local),
        grid=(local,),
        in_specs=[whole(g.shape) for g in gs]
        + [one(a.shape), one(b.shape), whole(pick.shape), whole(place.shape)]
        + [one(gate.shape), one(up.shape), one(down.shape)],
        out_specs=tuple(whole(o.shape) for o in outs),
        out_shape=outs,
        scratch_shapes=[
            pltpu.VMEM((local, rows, width), BF16),
            pltpu.VMEM((sources // 2, local, PAIR, width), BF16),
        ],
        compiler_params=pltpu.CompilerParams(vmem_limit_bytes=40 * 1024 * 1024),
        cost_estimate=pl.CostEstimate(
            flops=6 * local * rows * width * hidden,
            bytes_accessed=6 * local * width * hidden,
            transcendentals=0,
        ),
        name="backward",
    )(*gs, a, b, pick, place, gate, up, down)


def moved(value, by):
    count = lax.axis_size("expert")
    return lax.ppermute(value, "expert", [(i, (i + by) % count) for i in range(count)])


def swapped(value):
    return lax.ppermute(value, "expert", [(i, i ^ 1) for i in range(lax.axis_size("expert"))])


def moved_back(value, by):
    sections, count = lax.axis_size("section"), lax.axis_size("expert")
    pairs = [
        (s * count + i, ((s - 1) % sections) * count + (i + by) % count)
        for s in range(sections)
        for i in range(count)
    ]
    return lax.ppermute(value, ("section", "expert"), pairs)


def gathered(value):
    count = lax.axis_size("expert")
    if count != 4:
        return [value] + [moved(value, k) for k in range(1, count)]
    left, right = moved(value, 1), moved(value, -1)
    odd = lax.axis_index("expert") % 2 == 1
    far = swapped(jnp.where(odd, right, left))
    return [value, left, far, right]


def scattered(parts, kept, move):
    count = lax.axis_size("expert")
    if count != 4:
        sent = [(parts[k], -k) for k in range(1, count)]
    else:
        _, left, far, right = parts
        far = swapped(far).astype(F32)
        odd = lax.axis_index("expert") % 2 == 1
        added_left = (left.astype(F32) + far).astype(BF16)
        added_right = (right.astype(F32) + far).astype(BF16)
        sent = [(jnp.where(odd, left, added_left), -1), (jnp.where(odd, added_right, right), 1)]
    total = kept + parts[0]
    if move is moved_back:
        total = moved_back(total.astype(BF16), 0).astype(F32)
    for part, by in sent:
        total = total + move(part, by).astype(F32)
    return total.astype(BF16)


def shards(grad_out, saved_inputs, routes, gate_weights, w_gate, w_up, w_down):
    gate, up, down = w_gate[0], w_up[0], w_down[0]
    local = gate.shape[0]
    steps = routes.shape[1]
    base = (lax.axis_index("expert") * local).astype(jnp.int32).reshape(1)
    meta = jnp.concatenate(
        [routes[0].astype(F32).transpose(0, 2, 1), gate_weights[0].transpose(0, 2, 1)], axis=1
    )
    metas = gathered(meta)
    grad = grad_out[0]
    for step in range(steps):
        xs = gathered(saved_inputs[0, step])
        a, b, pick, place = forward(step, base, xs, metas, gate, up)
        gs = gathered(grad)
        parts = backward(gs, a, b, pick, place, gate, up, down)
        last = step + 1 == steps
        grad = scattered(parts, grad.astype(F32), moved if last else moved_back)
    return grad[None]


def solution(mesh):
    placed = (
        P("section", "expert", None),
        P("section", None, "expert", None),
        P("section", None, "expert", None),
        P("section", None, "expert", None),
        P("section", "expert", None, None),
        P("section", "expert", None, None),
        P("section", "expert", None, None),
    )
    return jax.shard_map(
        shards, mesh=mesh, in_specs=placed, out_specs=P("section", "expert", None), check_vma=False
    )
```

```python
import functools

import jax
import jax.numpy as jnp
from jax import lax
from jax.experimental import pallas as pl
from jax.experimental.pallas import tpu as pltpu
from jax.sharding import PartitionSpec as P

MOST = 40
PAIR = 2 * MOST
F32 = jnp.float32
BF16 = jnp.bfloat16


def dot(a, b, dims):
    return lax.dot_general(a, b, (dims, ((), ())), preferred_element_type=F32)


def expanded(local):
    slot = lax.broadcasted_iota(jnp.int32, (local, local * PAIR), 1)
    first = lax.broadcasted_iota(jnp.int32, (local, local * PAIR), 0) * PAIR
    return jnp.where((slot >= first) & (slot < first + PAIR), 1.0, 0.0).astype(BF16)


def forward_kernel(sources, local, tokens, step, base_ref, *refs):
    x_refs, refs = refs[:sources], refs[sources:]
    if step:
        meta_refs, refs = refs[:sources], refs[sources:]
    else:
        meta_refs = x_refs
    gate_ref, up_ref, a_ref, b_ref, pick_ref, place_ref, done_ref, rows_ref, weight_ref = refs
    top = x_refs[0].shape[1] // tokens

    mine = lax.broadcasted_iota(jnp.int32, (local, tokens), 0).astype(F32) + base_ref[0].astype(F32)
    before = (
        lax.broadcasted_iota(jnp.int32, (tokens, tokens), 0)
        < lax.broadcasted_iota(jnp.int32, (tokens, tokens), 1)
    )
    before = jnp.where(before, 1.0, 0.0).astype(BF16)
    table = expanded(local)
    for pair in range(sources // 2):
        targets, weights = [], []
        for half in range(2):
            meta = meta_refs[2 * pair + half][tokens:, :].astype(F32)[4 * step : 4 * step + 4]
            weights_of = meta[1:2] + meta[2:3] + meta[3:4]
            named = jnp.zeros((local, tokens), F32)
            weight = jnp.zeros((local, tokens), F32)
            for k in range(top):
                lanes = slice(k * tokens, (k + 1) * tokens)
                same = meta[0:1, lanes] == mine
                named = jnp.where(same, 1.0, named)
                weight = jnp.where(same, weights_of[:, lanes], weight)
            position = dot(named.astype(BF16), before, ((1,), (0,)))
            targets.append(jnp.where(named > 0.5, position + half * MOST, -1.0))
            weights.append(weight)
        target = jnp.concatenate(targets, axis=1).astype(BF16)
        weight = jnp.concatenate(weights, axis=1)
        spread = dot(table, target, ((0,), (0,)))
        slot = lax.broadcasted_iota(jnp.int32, spread.shape, 0) % PAIR
        picked = spread == slot.astype(F32)
        pick_ref[pair] = jnp.where(picked, 1.0, 0.0).astype(BF16)
        spread_t = dot(target, table, ((0,), (0,)))
        slot_t = lax.broadcasted_iota(jnp.int32, spread_t.shape, 1) % PAIR
        place_ref[pair] = jnp.where(spread_t == slot_t.astype(F32), 1.0, 0.0).astype(BF16)
        for e in range(local):
            block = jnp.where(picked[e * PAIR : (e + 1) * PAIR], weight[e : e + 1], 0.0)
            weight_ref[e, pair * PAIR : (pair + 1) * PAIR, :] = jnp.sum(block, axis=1, keepdims=True)
    pick_rows(x_refs, tokens, pick_ref, rows_ref)
    for e in range(local):
        rows = rows_ref[e]
        gate = dot(rows, gate_ref[e], ((1,), (1,)))
        up = dot(rows, up_ref[e], ((1,), (1,)))
        sig = 1.0 / (1.0 + jnp.exp(-gate))
        scaled = sig * weight_ref[e]
        a_ref[e] = up * scaled * (1.0 + gate * (1.0 - sig))
        b_ref[e] = gate * scaled
    done_ref[...] = jnp.zeros_like(done_ref)


def pick_rows(source_refs, tokens, pick_ref, rows_ref):
    local, width = rows_ref.shape[0], rows_ref.shape[2]
    for pair in range(len(source_refs) // 2):
        source = jnp.concatenate([ref[:tokens] for ref in source_refs[2 * pair : 2 * pair + 2]], axis=0)
        for n in range(0, width, 256):
            rows = dot(pick_ref[pair], source[:, n : n + 256], ((1,), (0,))).astype(BF16)
            rows_ref[:, pair * PAIR : (pair + 1) * PAIR, n : n + 256] = rows.reshape(local, PAIR, 256)


def backward_kernel(sources, local, *refs):
    g_refs, refs = refs[:sources], refs[sources:]
    a_ref, b_ref, pick_ref, place_ref, gate_ref, up_ref, down_ref = refs[:7]
    out_refs, refs = refs[7 : 7 + sources], refs[7 + sources :]
    rows_ref, back_ref = refs
    tokens, width = g_refs[0].shape

    pick_rows(g_refs, tokens, pick_ref, rows_ref)
    for e in range(local):
        hidden = dot(rows_ref[e], down_ref[e], ((1,), (0,)))
        gate_grad = (hidden * a_ref[e]).astype(BF16)
        up_grad = (hidden * b_ref[e]).astype(BF16)
        row = dot(gate_grad, gate_ref[e], ((1,), (0,))) + dot(up_grad, up_ref[e], ((1,), (0,)))
        row = row.astype(BF16)
        for pair in range(sources // 2):
            back_ref[pair, e] = row[pair * PAIR : (pair + 1) * PAIR]
    for pair in range(sources // 2):
        for n in range(0, width, 256):
            rows = back_ref[pair, :, :, n : n + 256].reshape(local * PAIR, 256)
            total = dot(place_ref[pair], rows, ((1,), (0,)))
            for half in range(2):
                out = out_refs[2 * pair + half]
                out[:, n : n + 256] = total[half * tokens : (half + 1) * tokens].astype(out.dtype)


def turn_kernel(*refs):
    e = pl.program_id(0)
    refs = refs[2:]
    count = len(refs) // 2
    for from_ref, to_ref in zip(refs[:count], refs[count:-1]):
        to_ref[e] = from_ref[0].T
    refs[-1][...] = jnp.zeros_like(refs[-1])


def first_kernel(saved_ref, grad_ref, routes_from, weights_from, out_ref, grad_out_ref, routes_ref, weights_ref, sems):
    tokens = saved_ref.shape[1]
    copies = [
        pltpu.make_async_copy(routes_from, routes_ref, sems.at[0]),
        pltpu.make_async_copy(weights_from, weights_ref, sems.at[1]),
        pltpu.make_async_copy(saved_ref.at[0], out_ref.at[:tokens], sems.at[2]),
        pltpu.make_async_copy(grad_ref, grad_out_ref, sems.at[3]),
    ]
    for copy in copies:
        copy.start()
    copies[0].wait()
    copies[1].wait()
    rows = []
    for step in range(routes_ref.shape[0]):
        weight = weights_ref[step]
        high = weight.astype(BF16).astype(F32)
        middle = (weight - high).astype(BF16).astype(F32)
        for part in (routes_ref[step].astype(F32), high, middle, weight - high - middle):
            rows.append(jnp.concatenate([part[k : k + 1] for k in range(part.shape[0])], axis=1))
    out_ref[tokens:] = jnp.concatenate(rows, axis=0).astype(BF16)
    copies[2].wait()
    copies[3].wait()


VMEM = pl.BlockSpec(memory_space=pltpu.VMEM)
MIB = 1024 * 1024
SMALL = pl.CostEstimate(flops=0, bytes_accessed=1024, transcendentals=0)
DONE = pltpu.VMEM((8, 128), F32)


def near(*values):
    return [pltpu.with_memory_space_constraint(v, pltpu.VMEM) for v in values]


def one(shape):
    return pl.BlockSpec((1,) + shape[1:], lambda e: (e,) + (0,) * (len(shape) - 1))


def turned(who, *weights):
    local = weights[0].shape[0]
    shapes = [(local, w.shape[2], w.shape[1]) for w in weights]
    return pl.pallas_call(
        turn_kernel,
        grid=(local,),
        in_specs=[pl.BlockSpec(memory_space=pltpu.SMEM)] * 2 + [one(w.shape) for w in weights],
        out_specs=(VMEM,) * (len(weights) + 1),
        out_shape=(*[pltpu.VMEM(shape, BF16) for shape in shapes], DONE),
        compiler_params=pltpu.CompilerParams(vmem_limit_bytes=10 * MIB),
        cost_estimate=SMALL,
        name="turn",
    )(*who, *[pltpu.with_memory_space_constraint(w, pltpu.HBM) for w in weights])


def first_blocks(saved, grad, routes, weights):
    steps, tokens, width = saved.shape
    return pl.pallas_call(
        first_kernel,
        in_specs=[pl.BlockSpec(memory_space=pl.ANY)] * 4,
        out_specs=(VMEM,) * 2,
        out_shape=(pltpu.VMEM((tokens + 4 * steps, width), BF16), pltpu.VMEM(grad.shape, BF16)),
        scratch_shapes=[
            pltpu.VMEM(routes.shape, routes.dtype),
            pltpu.VMEM(weights.shape, weights.dtype),
            pltpu.SemaphoreType.DMA((4,)),
        ],
        compiler_params=pltpu.CompilerParams(vmem_limit_bytes=4 * MIB),
        cost_estimate=SMALL,
        name="first",
    )(*[pltpu.with_memory_space_constraint(v, pltpu.HBM) for v in (saved, grad, routes, weights)])


def choose_kernel(odd_ref, done_ref, left_ref, right_ref, out_ref):
    @pl.when(odd_ref[0] == 1)
    def _():
        out_ref[...] = right_ref[...]

    @pl.when(odd_ref[0] == 0)
    def _():
        out_ref[...] = left_ref[...]


def chosen(who, done, left, right):
    done = left if done is who[1] else done
    return pl.pallas_call(
        choose_kernel,
        in_specs=[pl.BlockSpec(memory_space=pltpu.SMEM)] + [VMEM] * 3,
        out_specs=VMEM,
        out_shape=pltpu.VMEM(left.shape, left.dtype),
        compiler_params=pltpu.CompilerParams(vmem_limit_bytes=4 * MIB),
        cost_estimate=SMALL,
        name="choose",
    )(who[1], *near(done, left, right))


def join_kernel(odd_ref, far_ref, left_ref, right_ref, *refs):
    to_left_ref, to_right_ref = refs[-2:]
    far = far_ref[...].astype(F32)

    @pl.when(odd_ref[0] == 1)
    def _():
        to_left_ref[...] = left_ref[...]
        to_right_ref[...] = (right_ref[...].astype(F32) + far).astype(BF16)

    @pl.when(odd_ref[0] == 0)
    def _():
        to_left_ref[...] = (left_ref[...].astype(F32) + far).astype(BF16)
        to_right_ref[...] = right_ref[...]


def joined(who, far, left, right, beside):
    return pl.pallas_call(
        join_kernel,
        in_specs=[pl.BlockSpec(memory_space=pltpu.SMEM)] + [VMEM] * (3 + len(beside)),
        out_specs=(VMEM,) * 2,
        out_shape=(pltpu.VMEM(left.shape, left.dtype),) * 2,
        compiler_params=pltpu.CompilerParams(vmem_limit_bytes=4 * MIB),
        cost_estimate=SMALL,
        name="join",
    )(who[1], *near(far, left, right, *beside))


def later_kernel(index, saved_ref, done_ref, out_ref, sem):
    copy = pltpu.make_async_copy(saved_ref.at[index], out_ref, sem)
    copy.start()
    copy.wait()


def later_block(saved, index, done):
    return pl.pallas_call(
        functools.partial(later_kernel, index),
        in_specs=[pl.BlockSpec(memory_space=pl.ANY), VMEM],
        out_specs=VMEM,
        out_shape=pltpu.VMEM(saved.shape[1:], saved.dtype),
        scratch_shapes=[pltpu.SemaphoreType.DMA],
        compiler_params=pltpu.CompilerParams(vmem_limit_bytes=4 * MIB),
        cost_estimate=SMALL,
        name="later",
    )(pltpu.with_memory_space_constraint(saved, pltpu.HBM), *near(done))


def forward(step, who, tokens, xs, metas, gate, up):
    sources, local = len(xs), gate.shape[0]
    width = xs[0].shape[1]
    hidden = gate.shape[1]
    rows = sources * MOST
    arrays = (*xs, *metas, gate, up) if step else (*xs, gate, up)
    return pl.pallas_call(
        functools.partial(forward_kernel, sources, local, tokens, step),
        in_specs=[pl.BlockSpec(memory_space=pltpu.SMEM)] + [VMEM] * len(arrays),
        out_specs=(VMEM,) * 5,
        out_shape=(
            pltpu.VMEM((local, rows, hidden), F32),
            pltpu.VMEM((local, rows, hidden), F32),
            pltpu.VMEM((sources // 2, local * PAIR, 2 * tokens), BF16),
            pltpu.VMEM((sources // 2, 2 * tokens, local * PAIR), BF16),
            DONE,
        ),
        scratch_shapes=[
            pltpu.VMEM((local, rows, width), BF16),
            pltpu.VMEM((local, rows, 1), F32),
        ],
        compiler_params=pltpu.CompilerParams(vmem_limit_bytes=11 * MIB),
        cost_estimate=SMALL,
        name="forward",
    )(who[0], *near(*arrays))


def backward(gs, a, b, pick, place, gate, up, down):
    sources, local = len(gs), gate.shape[0]
    tokens, width = gs[0].shape
    hidden = gate.shape[1]
    rows = sources * MOST
    outs = tuple(pltpu.VMEM((tokens, width), F32 if k == 0 else BF16) for k in range(sources))
    return pl.pallas_call(
        functools.partial(backward_kernel, sources, local),
        in_specs=[VMEM] * (sources + 7),
        out_specs=(VMEM,) * sources,
        out_shape=outs,
        scratch_shapes=[
            pltpu.VMEM((local, rows, width), BF16),
            pltpu.VMEM((sources // 2, local, PAIR, width), BF16),
        ],
        compiler_params=pltpu.CompilerParams(vmem_limit_bytes=13 * MIB),
        cost_estimate=SMALL,
        name="backward",
    )(*near(*gs, a, b, pick, place, gate, up, down))


def moved(value, by):
    count = lax.axis_size("expert")
    return lax.ppermute(value, "expert", [(i, (i + by) % count) for i in range(count)])


def swapped(value):
    return lax.ppermute(value, "expert", [(i, i ^ 1) for i in range(lax.axis_size("expert"))])


def moved_back(value, by):
    sections, count = lax.axis_size("section"), lax.axis_size("expert")
    pairs = [
        (s * count + i, ((s - 1) % sections) * count + (i + by) % count)
        for s in range(sections)
        for i in range(count)
    ]
    return lax.ppermute(value, ("section", "expert"), pairs)


def gathered_near(value):
    count = lax.axis_size("expert")
    if count != 4:
        return [value] + [moved(value, k) for k in range(1, count)]
    return [value, moved(value, 1), None, moved(value, -1)]


def gathered_far(who, blocks, done):
    if blocks[2] is not None:
        return blocks
    value, left, _, right = blocks
    return [value, left, swapped(chosen(who, done, left, right)), right]


def scattered(who, parts, kept, move, beside, done):
    count = lax.axis_size("expert")
    if count != 4:
        sent = [(parts[k], -k) for k in range(1, count)]
    else:
        own, left, far, right = parts
        far = swapped(far)
        to_left, to_right = joined(who, far, left, right, beside[1::2] if beside else ())
        if beside is not None:
            beside = gathered_far(who, beside, done)
        sent = [(to_left, -1), (to_right, 1)]
    total = kept + parts[0]
    if move is moved_back:
        total = moved_back(total.astype(BF16), 0).astype(F32)
    for part, by in sent:
        total = total + move(part, by).astype(F32)
    return total.astype(BF16), beside


def shards(grad_out, saved_inputs, routes, gate_weights, w_gate, w_up, w_down):
    gate, up, down = w_gate[0], w_up[0], w_down[0]
    local = gate.shape[0]
    tokens = grad_out.shape[1]
    steps = routes.shape[1]
    place = lax.axis_index("expert").astype(jnp.int32)
    who = ((place * local).reshape(1), (place % 2).reshape(1))
    first, grad = first_blocks(
        saved_inputs[0], grad_out[0], routes[0].transpose(0, 2, 1), gate_weights[0].transpose(0, 2, 1)
    )
    xs = gathered_near(first)
    gs = gathered_near(grad)
    *back, done = turned(who, gate, up, down)
    xs = gathered_far(who, xs, who[1])
    metas = xs
    for step in range(steps):
        last = step + 1 == steps
        if step == 0:
            gs = gathered_far(who, gs, done)
        *factors, done = forward(step, who, tokens, xs, metas, back[0], back[1])
        if step:
            gs = gathered_far(who, gs, done)
        beside = None
        if not last:
            beside = gathered_near(later_block(saved_inputs[0], step + 1, done))
        parts = backward(gs, *factors, *back)
        grad, xs = scattered(
            who, parts, grad.astype(F32), moved if last else moved_back, beside, done
        )
        if not last:
            gs = gathered_near(grad)
    return grad[None]


def solution(mesh):
    placed = (
        P("section", "expert", None),
        P("section", None, "expert", None),
        P("section", None, "expert", None),
        P("section", None, "expert", None),
        P("section", "expert", None, None),
        P("section", "expert", None, None),
        P("section", "expert", None, None),
    )
    return jax.shard_map(
        shards, mesh=mesh, in_specs=placed, out_specs=P("section", "expert", None), check_vma=False
    )
```

```python
import functools

import jax
import jax.numpy as jnp
from jax import lax
from jax.experimental import pallas as pl
from jax.experimental.pallas import tpu as pltpu
from jax.sharding import PartitionSpec as P

MOST = 40
PAIR = 2 * MOST
F32 = jnp.float32
BF16 = jnp.bfloat16


def dot(a, b, dims):
    return lax.dot_general(a, b, (dims, ((), ())), preferred_element_type=F32)


def expanded(local):
    slot = lax.broadcasted_iota(jnp.int32, (local, local * PAIR), 1)
    first = lax.broadcasted_iota(jnp.int32, (local, local * PAIR), 0) * PAIR
    return jnp.where((slot >= first) & (slot < first + PAIR), 1.0, 0.0).astype(BF16)


def forward_kernel(sources, local, tokens, step, base_ref, *refs):
    x_refs, refs = refs[:sources], refs[sources:]
    if step:
        meta_refs, refs = refs[:sources], refs[sources:]
    else:
        meta_refs = x_refs
    gate_ref, up_ref, a_ref, b_ref, pick_ref, place_ref, done_ref, rows_ref, weight_ref = refs
    top = x_refs[0].shape[1] // tokens

    mine = lax.broadcasted_iota(jnp.int32, (local, tokens), 0).astype(F32) + base_ref[0].astype(F32)
    before = (
        lax.broadcasted_iota(jnp.int32, (tokens, tokens), 0)
        < lax.broadcasted_iota(jnp.int32, (tokens, tokens), 1)
    )
    before = jnp.where(before, 1.0, 0.0).astype(BF16)
    table = expanded(local)
    for pair in range(sources // 2):
        targets, weights = [], []
        for half in range(2):
            meta = meta_refs[2 * pair + half][tokens:, :].astype(F32)[4 * step : 4 * step + 4]
            weights_of = meta[1:2] + meta[2:3] + meta[3:4]
            named = jnp.zeros((local, tokens), F32)
            weight = jnp.zeros((local, tokens), F32)
            for k in range(top):
                lanes = slice(k * tokens, (k + 1) * tokens)
                same = meta[0:1, lanes] == mine
                named = jnp.where(same, 1.0, named)
                weight = jnp.where(same, weights_of[:, lanes], weight)
            position = dot(named.astype(BF16), before, ((1,), (0,)))
            targets.append(jnp.where(named > 0.5, position + half * MOST, -1.0))
            weights.append(weight)
        target = jnp.concatenate(targets, axis=1).astype(BF16)
        weight = jnp.concatenate(weights, axis=1)
        spread = dot(table, target, ((0,), (0,)))
        slot = lax.broadcasted_iota(jnp.int32, spread.shape, 0) % PAIR
        picked = spread == slot.astype(F32)
        pick_ref[pair] = jnp.where(picked, 1.0, 0.0).astype(BF16)
        spread_t = dot(target, table, ((0,), (0,)))
        slot_t = lax.broadcasted_iota(jnp.int32, spread_t.shape, 1) % PAIR
        place_ref[pair] = jnp.where(spread_t == slot_t.astype(F32), 1.0, 0.0).astype(BF16)
        for e in range(local):
            block = jnp.where(picked[e * PAIR : (e + 1) * PAIR], weight[e : e + 1], 0.0)
            weight_ref[e, pair * PAIR : (pair + 1) * PAIR, :] = jnp.sum(block, axis=1, keepdims=True)
    pick_rows(x_refs, tokens, pick_ref, rows_ref)
    for e in range(local):
        rows = rows_ref[e]
        gate = dot(rows, gate_ref[e], ((1,), (1,)))
        up = dot(rows, up_ref[e], ((1,), (1,)))
        sig = 1.0 / (1.0 + jnp.exp(-gate))
        scaled = sig * weight_ref[e]
        a_ref[e] = up * scaled * (1.0 + gate * (1.0 - sig))
        b_ref[e] = gate * scaled
    done_ref[...] = jnp.zeros_like(done_ref)


def pick_rows(source_refs, tokens, pick_ref, rows_ref):
    local, width = rows_ref.shape[0], rows_ref.shape[2]
    for pair in range(len(source_refs) // 2):
        source = jnp.concatenate([ref[:tokens] for ref in source_refs[2 * pair : 2 * pair + 2]], axis=0)
        for n in range(0, width, 256):
            rows = dot(pick_ref[pair], source[:, n : n + 256], ((1,), (0,))).astype(BF16)
            rows_ref[:, pair * PAIR : (pair + 1) * PAIR, n : n + 256] = rows.reshape(local, PAIR, 256)


def pick_pieces(sources, pieces, piece_refs, pick_ref, rows_ref):
    start = 0
    for piece in range(pieces):
        refs = [piece_refs[k * pieces + piece] for k in range(sources)]
        tokens, width = refs[0].shape
        pick_rows(refs, tokens, pick_ref, rows_ref.at[:, :, start : start + width])
        start += width


def row_piece(kept_ref, gate_grad_ref, up_grad_ref, place_ref, gate_ref, up_ref, out_refs, back_ref, columns):
    local = gate_ref.shape[0]
    pairs, double = place_ref.shape[0], place_ref.shape[1]
    tokens = double // 2
    for e in range(local):
        row = dot(gate_grad_ref[e], gate_ref[e, :, columns], ((1,), (0,)))
        row = (row + dot(up_grad_ref[e], up_ref[e, :, columns], ((1,), (0,)))).astype(BF16)
        for pair in range(pairs):
            back_ref[pair, e] = row[pair * PAIR : (pair + 1) * PAIR]
    width = columns.stop - columns.start
    for pair in range(pairs):
        for n in range(0, width, 256):
            rows = back_ref[pair, :, :, n : n + 256].reshape(local * PAIR, 256)
            total = dot(place_ref[pair], rows, ((1,), (0,)))
            for half in range(2):
                out = out_refs[2 * pair + half]
                part = total[half * tokens : (half + 1) * tokens]
                if pair == 0 and half == 0:
                    first = columns.start if kept_ref.shape[1] > width else 0
                    part = part + kept_ref[:, first + n : first + n + 256].astype(F32)
                out[:, n : n + 256] = part.astype(out.dtype)


def backward_kernel(sources, pieces, columns, *refs):
    g_refs, refs = refs[: sources * pieces], refs[sources * pieces :]
    a_ref, b_ref, pick_ref, place_ref, gate_ref, up_ref, down_ref = refs[:7]
    out_refs, refs = refs[7 : 7 + sources], refs[7 + sources :]
    gate_grad_ref, up_grad_ref, rows_ref, back_ref = refs
    pick_pieces(sources, pieces, g_refs, pick_ref, rows_ref)
    for e in range(rows_ref.shape[0]):
        hidden = dot(rows_ref[e], down_ref[e], ((1,), (0,)))
        gate_grad_ref[e] = (hidden * a_ref[e]).astype(BF16)
        up_grad_ref[e] = (hidden * b_ref[e]).astype(BF16)
    row_piece(g_refs[0], gate_grad_ref, up_grad_ref, place_ref, gate_ref, up_ref, out_refs, back_ref, columns)


def rest_kernel(sources, columns, kept_ref, gate_grad_ref, up_grad_ref, place_ref, gate_ref, up_ref, *refs):
    row_piece(
        kept_ref, gate_grad_ref, up_grad_ref, place_ref, gate_ref, up_ref, refs[:sources], refs[sources], columns
    )


def hold_kernel(index, value_ref, *refs):
    refs[-1][...] = value_ref[index]


def turn_kernel(*refs):
    e = pl.program_id(0)
    refs = refs[3:]
    count = len(refs) // 2
    for from_ref, to_ref in zip(refs[:count], refs[count:-1]):
        to_ref[e] = from_ref[0].T
    refs[-1][...] = jnp.zeros_like(refs[-1])


def first_kernel(saved_ref, grad_ref, routes_from, weights_from, out_ref, grad_out_ref, routes_ref, weights_ref, sems):
    tokens = saved_ref.shape[1]
    copies = [
        pltpu.make_async_copy(routes_from, routes_ref, sems.at[0]),
        pltpu.make_async_copy(weights_from, weights_ref, sems.at[1]),
        pltpu.make_async_copy(saved_ref.at[0], out_ref.at[:tokens], sems.at[2]),
        pltpu.make_async_copy(grad_ref, grad_out_ref, sems.at[3]),
    ]
    for copy in copies:
        copy.start()
    copies[0].wait()
    copies[1].wait()
    rows = []
    for step in range(routes_ref.shape[0]):
        weight = weights_ref[step]
        high = weight.astype(BF16).astype(F32)
        middle = (weight - high).astype(BF16).astype(F32)
        for part in (routes_ref[step].astype(F32), high, middle, weight - high - middle):
            rows.append(jnp.concatenate([part[k : k + 1] for k in range(part.shape[0])], axis=1))
    out_ref[tokens:] = jnp.concatenate(rows, axis=0).astype(BF16)
    for copy in copies[2:]:
        copy.wait()


VMEM = pl.BlockSpec(memory_space=pltpu.VMEM)
MIB = 1024 * 1024
SMALL = pl.CostEstimate(flops=0, bytes_accessed=1024, transcendentals=0)
DONE = pltpu.VMEM((8, 128), F32)


def near(*values):
    return [pltpu.with_memory_space_constraint(v, pltpu.VMEM) for v in values]


def one(shape):
    return pl.BlockSpec((1,) + shape[1:], lambda e: (e,) + (0,) * (len(shape) - 1))


def turned(who, after, *weights):
    local = weights[0].shape[0]
    shapes = [(local, w.shape[2], w.shape[1]) for w in weights]
    return pl.pallas_call(
        turn_kernel,
        grid=(local,),
        in_specs=[pl.BlockSpec(memory_space=pltpu.SMEM)] * 2 + [VMEM] + [one(w.shape) for w in weights],
        out_specs=(VMEM,) * (len(weights) + 1),
        out_shape=(*[pltpu.VMEM(shape, BF16) for shape in shapes], DONE),
        compiler_params=pltpu.CompilerParams(vmem_limit_bytes=10 * MIB),
        cost_estimate=SMALL,
        name="turn",
    )(*who, *near(after), *[pltpu.with_memory_space_constraint(w, pltpu.HBM) for w in weights])


def first_blocks(saved, grad, routes, weights):
    steps, tokens, width = saved.shape
    return pl.pallas_call(
        first_kernel,
        in_specs=[pl.BlockSpec(memory_space=pl.ANY)] * 4,
        out_specs=(VMEM,) * 2,
        out_shape=(pltpu.VMEM((tokens + 4 * steps, width), BF16), pltpu.VMEM(grad.shape, BF16)),
        scratch_shapes=[
            pltpu.VMEM(routes.shape, routes.dtype),
            pltpu.VMEM(weights.shape, weights.dtype),
            pltpu.SemaphoreType.DMA((4,)),
        ],
        compiler_params=pltpu.CompilerParams(vmem_limit_bytes=2 * MIB),
        cost_estimate=SMALL,
        name="first",
    )(*[pltpu.with_memory_space_constraint(v, pltpu.HBM) for v in (saved, grad, routes, weights)])


def choose_kernel(odd_ref, done_ref, left_ref, right_ref, out_ref):
    @pl.when(odd_ref[0] == 1)
    def _():
        out_ref[...] = right_ref[...]

    @pl.when(odd_ref[0] == 0)
    def _():
        out_ref[...] = left_ref[...]


def chosen(who, done, left, right):
    done = left if done is who[1] else done
    return pl.pallas_call(
        choose_kernel,
        in_specs=[pl.BlockSpec(memory_space=pltpu.SMEM)] + [VMEM] * 3,
        out_specs=VMEM,
        out_shape=pltpu.VMEM(left.shape, left.dtype),
        compiler_params=pltpu.CompilerParams(vmem_limit_bytes=2 * MIB),
        cost_estimate=SMALL,
        name="choose",
    )(who[1], *near(done, left, right))


def join_kernel(odd_ref, far_ref, left_ref, right_ref, *refs):
    to_left_ref, to_right_ref = refs[-2:]
    far = far_ref[...].astype(F32)

    @pl.when(odd_ref[0] == 1)
    def _():
        to_left_ref[...] = left_ref[...]
        to_right_ref[...] = (right_ref[...].astype(F32) + far).astype(BF16)

    @pl.when(odd_ref[0] == 0)
    def _():
        to_left_ref[...] = (left_ref[...].astype(F32) + far).astype(BF16)
        to_right_ref[...] = right_ref[...]


def joined(who, far, left, right, beside):
    return pl.pallas_call(
        join_kernel,
        in_specs=[pl.BlockSpec(memory_space=pltpu.SMEM)] + [VMEM] * (3 + len(beside)),
        out_specs=(VMEM,) * 2,
        out_shape=(pltpu.VMEM(left.shape, left.dtype),) * 2,
        compiler_params=pltpu.CompilerParams(vmem_limit_bytes=2 * MIB),
        cost_estimate=SMALL,
        name="join",
    )(who[1], *near(far, left, right, *beside))


def held(value, index, *after):
    return pl.pallas_call(
        functools.partial(hold_kernel, index),
        in_specs=[VMEM] * (1 + len(after)),
        out_specs=VMEM,
        out_shape=pltpu.VMEM(value.shape[1:], value.dtype),
        compiler_params=pltpu.CompilerParams(vmem_limit_bytes=2 * MIB),
        cost_estimate=SMALL,
        name="hold",
    )(*near(value, *after))


def forward(step, who, tokens, xs, metas, gate, up):
    sources, local = len(xs), gate.shape[0]
    width = xs[0].shape[1]
    hidden = gate.shape[1]
    rows = sources * MOST
    arrays = (*xs, *metas, gate, up) if step else (*xs, gate, up)
    return pl.pallas_call(
        functools.partial(forward_kernel, sources, local, tokens, step),
        in_specs=[pl.BlockSpec(memory_space=pltpu.SMEM)] + [VMEM] * len(arrays),
        out_specs=(VMEM,) * 5,
        out_shape=(
            pltpu.VMEM((local, rows, hidden), F32),
            pltpu.VMEM((local, rows, hidden), F32),
            pltpu.VMEM((sources // 2, local * PAIR, 2 * tokens), BF16),
            pltpu.VMEM((sources // 2, 2 * tokens, local * PAIR), BF16),
            DONE,
        ),
        scratch_shapes=[
            pltpu.VMEM((local, rows, width), BF16),
            pltpu.VMEM((local, rows, 1), F32),
        ],
        compiler_params=pltpu.CompilerParams(vmem_limit_bytes=9 * MIB),
        cost_estimate=SMALL,
        name="forward",
    )(who[0], *near(*arrays))


def backward(gs, a, b, pick, place, gate, up, down, kept_type):
    sources, pieces, local = len(gs), len(gs[0]), gate.shape[0]
    tokens = gs[0][0].shape[0]
    hidden, width = gate.shape[1:]
    rows = sources * MOST
    half = width // 2
    types = [kept_type] + [BF16] * (sources - 1)
    outs = tuple(pltpu.VMEM((tokens, half), t) for t in types)
    factor = pltpu.VMEM((local, rows, hidden), BF16)
    back = pltpu.VMEM((sources // 2, local, PAIR, half), BF16)
    *first, gate_grad, up_grad = pl.pallas_call(
        functools.partial(backward_kernel, sources, pieces, slice(0, half)),
        in_specs=[VMEM] * (sources * pieces + 7),
        out_specs=(VMEM,) * (sources + 2),
        out_shape=outs + (factor, factor),
        scratch_shapes=[pltpu.VMEM((local, rows, width), BF16), back],
        compiler_params=pltpu.CompilerParams(vmem_limit_bytes=11 * MIB),
        cost_estimate=SMALL,
        name="backward",
    )(*near(*[g for block in gs for g in block], a, b, pick, place, gate, up, down))
    rest = pl.pallas_call(
        functools.partial(rest_kernel, sources, slice(half, width)),
        in_specs=[VMEM] * 6,
        out_specs=(VMEM,) * sources,
        out_shape=outs,
        scratch_shapes=[back],
        compiler_params=pltpu.CompilerParams(vmem_limit_bytes=6 * MIB),
        cost_estimate=SMALL,
        name="rest",
    )(*near(gs[0][-1], gate_grad, up_grad, place, gate, up))
    return first, rest


def moved(value, by):
    count = lax.axis_size("expert")
    return lax.ppermute(value, "expert", [(i, (i + by) % count) for i in range(count)])


def swapped(value):
    return lax.ppermute(value, "expert", [(i, i ^ 1) for i in range(lax.axis_size("expert"))])


def moved_back(value, by):
    sections, count = lax.axis_size("section"), lax.axis_size("expert")
    pairs = [
        (s * count + i, ((s - 1) % sections) * count + (i + by) % count)
        for s in range(sections)
        for i in range(count)
    ]
    return lax.ppermute(value, ("section", "expert"), pairs)


def gathered_near(value):
    count = lax.axis_size("expert")
    if count != 4:
        return [value] + [moved(value, k) for k in range(1, count)]
    return [value, moved(value, 1), None, moved(value, -1)]


def gathered_far(who, blocks, done):
    if blocks[2] is not None:
        return blocks, None
    value, left, _, right = blocks
    passed = chosen(who, done, left, right)
    return [value, left, swapped(passed), right], passed


def joined_parts(who, parts, beside):
    if lax.axis_size("expert") != 4:
        return [(parts[k], -k) for k in range(1, len(parts))]
    _, left, far, right = parts
    to_left, to_right = joined(who, swapped(far), left, right, beside)
    return [(to_left, -1), (to_right, 1)]


def scattered(own, sent, last):
    move = moved if last else moved_back
    total = own if last else move(own, 0).astype(F32)
    for part, by in sent:
        total = total + move(part, by).astype(F32)
    return total.astype(BF16)


def shards(grad_out, saved_inputs, routes, gate_weights, w_gate, w_up, w_down):
    gate, up, down = w_gate[0], w_up[0], w_down[0]
    local = gate.shape[0]
    tokens = grad_out.shape[1]
    steps = routes.shape[1]
    ringed = lax.axis_size("expert") == 4
    place = lax.axis_index("expert").astype(jnp.int32)
    who = ((place * local).reshape(1), (place % 2).reshape(1))
    first, grad = first_blocks(
        saved_inputs[0], grad_out[0], routes[0].transpose(0, 2, 1), gate_weights[0].transpose(0, 2, 1)
    )
    xs = gathered_near(first)
    gs = gathered_near(grad)
    xs, passed = gathered_far(who, xs, first)
    metas = xs
    *back, done = turned(who, passed if ringed else first, gate, up, down)
    gs = [[g] for g in gathered_far(who, gs, done)[0]]
    for step in range(steps):
        last = step + 1 == steps
        *factors, done = forward(step, who, tokens, xs, metas, back[0], back[1])
        if step:
            gs = [list(block) for block in zip(*[gathered_far(who, g, done)[0] for g in gs])]
        beside = ()
        if not last:
            following = held(saved_inputs[0], step + 1, gs[-2][0], done) if ringed else saved_inputs[0, step + 1]
            xs = gathered_near(following)
            beside = xs[1::2] if ringed else ()
        halves = backward(gs, *factors, *back, F32 if last else BF16)
        sent = [joined_parts(who, parts, beside) for parts in halves]
        grads = [scattered(parts[0], pairs, last) for parts, pairs in zip(halves, sent)]
        if not last:
            xs, _ = gathered_far(who, xs, done)
            gs = [gathered_near(grad) for grad in grads]
    return jnp.concatenate(grads, axis=1)[None]


def solution(mesh):
    placed = (
        P("section", "expert", None),
        P("section", None, "expert", None),
        P("section", None, "expert", None),
        P("section", None, "expert", None),
        P("section", "expert", None, None),
        P("section", "expert", None, None),
        P("section", "expert", None, None),
    )
    return jax.shard_map(
        shards, mesh=mesh, in_specs=placed, out_specs=P("section", "expert", None), check_vma=False
    )
```

```python
import functools

import jax
import jax.numpy as jnp
from jax import lax
from jax.experimental import pallas as pl
from jax.experimental.pallas import tpu as pltpu
from jax.sharding import PartitionSpec as P

MOST = 40
PAIR = 2 * MOST
F32 = jnp.float32
BF16 = jnp.bfloat16


def dot(a, b, dims):
    return lax.dot_general(a, b, (dims, ((), ())), preferred_element_type=F32)


def expanded(local):
    slot = lax.broadcasted_iota(jnp.int32, (local, local * PAIR), 1)
    first = lax.broadcasted_iota(jnp.int32, (local, local * PAIR), 0) * PAIR
    return jnp.where((slot >= first) & (slot < first + PAIR), 1.0, 0.0).astype(BF16)


def forward_kernel(sources, local, tokens, step, base_ref, *refs):
    x_refs, refs = refs[:sources], refs[sources:]
    if step:
        meta_refs, refs = refs[:sources], refs[sources:]
    else:
        meta_refs = x_refs
    gate_ref, up_ref, a_ref, b_ref, pick_ref, place_ref, done_ref, rows_ref, weight_ref = refs
    top = x_refs[0].shape[1] // tokens

    mine = lax.broadcasted_iota(jnp.int32, (local, tokens), 0).astype(F32) + base_ref[0].astype(F32)
    before = (
        lax.broadcasted_iota(jnp.int32, (tokens, tokens), 0)
        < lax.broadcasted_iota(jnp.int32, (tokens, tokens), 1)
    )
    before = jnp.where(before, 1.0, 0.0).astype(BF16)
    table = expanded(local)
    for pair in range(sources // 2):
        targets, weights = [], []
        for half in range(2):
            meta = meta_refs[2 * pair + half][tokens:, :].astype(F32)[4 * step : 4 * step + 4]
            weights_of = meta[1:2] + meta[2:3] + meta[3:4]
            named = jnp.zeros((local, tokens), F32)
            weight = jnp.zeros((local, tokens), F32)
            for k in range(top):
                lanes = slice(k * tokens, (k + 1) * tokens)
                same = meta[0:1, lanes] == mine
                named = jnp.where(same, 1.0, named)
                weight = jnp.where(same, weights_of[:, lanes], weight)
            position = dot(named.astype(BF16), before, ((1,), (0,)))
            targets.append(jnp.where(named > 0.5, position + half * MOST, -1.0))
            weights.append(weight)
        target = jnp.concatenate(targets, axis=1).astype(BF16)
        weight = jnp.concatenate(weights, axis=1)
        spread = dot(table, target, ((0,), (0,)))
        slot = lax.broadcasted_iota(jnp.int32, spread.shape, 0) % PAIR
        picked = spread == slot.astype(F32)
        pick_ref[pair] = jnp.where(picked, 1.0, 0.0).astype(BF16)
        spread_t = dot(target, table, ((0,), (0,)))
        slot_t = lax.broadcasted_iota(jnp.int32, spread_t.shape, 1) % PAIR
        place_ref[pair] = jnp.where(spread_t == slot_t.astype(F32), 1.0, 0.0).astype(BF16)
        for e in range(local):
            block = jnp.where(picked[e * PAIR : (e + 1) * PAIR], weight[e : e + 1], 0.0)
            weight_ref[e, pair * PAIR : (pair + 1) * PAIR, :] = jnp.sum(block, axis=1, keepdims=True)
    pick_rows(x_refs, tokens, pick_ref, rows_ref)
    for e in range(local):
        rows = rows_ref[e]
        gate = dot(rows, gate_ref[e], ((1,), (1,)))
        up = dot(rows, up_ref[e], ((1,), (1,)))
        sig = 1.0 / (1.0 + jnp.exp(-gate))
        scaled = sig * weight_ref[e]
        a_ref[e] = up * scaled * (1.0 + gate * (1.0 - sig))
        b_ref[e] = gate * scaled
    done_ref[...] = jnp.zeros_like(done_ref)


def pick_rows(source_refs, tokens, pick_ref, rows_ref):
    local, width = rows_ref.shape[0], rows_ref.shape[2]
    for pair in range(len(source_refs) // 2):
        source = jnp.concatenate([ref[:tokens] for ref in source_refs[2 * pair : 2 * pair + 2]], axis=0)
        for n in range(0, width, 256):
            rows = dot(pick_ref[pair], source[:, n : n + 256], ((1,), (0,))).astype(BF16)
            rows_ref[:, pair * PAIR : (pair + 1) * PAIR, n : n + 256] = rows.reshape(local, PAIR, 256)


def pick_pieces(sources, pieces, piece_refs, pick_ref, rows_ref):
    start = 0
    for piece in range(pieces):
        refs = [piece_refs[k * pieces + piece] for k in range(sources)]
        tokens, width = refs[0].shape
        pick_rows(refs, tokens, pick_ref, rows_ref.at[:, :, start : start + width])
        start += width


def row_piece(kept_ref, gate_grad_ref, up_grad_ref, place_ref, gate_ref, up_ref, out_refs, back_ref, columns):
    local = gate_ref.shape[0]
    pairs, double = place_ref.shape[0], place_ref.shape[1]
    tokens = double // 2
    for e in range(local):
        row = dot(gate_grad_ref[e], gate_ref[e, :, columns], ((1,), (0,)))
        row = (row + dot(up_grad_ref[e], up_ref[e, :, columns], ((1,), (0,)))).astype(BF16)
        for pair in range(pairs):
            back_ref[pair, e] = row[pair * PAIR : (pair + 1) * PAIR]
    width = columns.stop - columns.start
    for pair in range(pairs):
        for n in range(0, width, 256):
            rows = back_ref[pair, :, :, n : n + 256].reshape(local * PAIR, 256)
            total = dot(place_ref[pair], rows, ((1,), (0,)))
            for half in range(2):
                out = out_refs[2 * pair + half]
                part = total[half * tokens : (half + 1) * tokens]
                if pair == 0 and half == 0:
                    first = columns.start if kept_ref.shape[1] > width else 0
                    part = part + kept_ref[:, first + n : first + n + 256].astype(F32)
                out[:, n : n + 256] = part.astype(out.dtype)


def backward_kernel(sources, pieces, columns, *refs):
    g_refs, refs = refs[: sources * pieces], refs[sources * pieces :]
    a_ref, b_ref, pick_ref, place_ref, gate_ref, up_ref, down_ref = refs[:7]
    out_refs, refs = refs[7 : 7 + sources], refs[7 + sources :]
    gate_grad_ref, up_grad_ref, rows_ref, back_ref = refs
    pick_pieces(sources, pieces, g_refs, pick_ref, rows_ref)
    for e in range(rows_ref.shape[0]):
        hidden = dot(rows_ref[e], down_ref[e], ((1,), (0,)))
        gate_grad_ref[e] = (hidden * a_ref[e]).astype(BF16)
        up_grad_ref[e] = (hidden * b_ref[e]).astype(BF16)
    row_piece(g_refs[0], gate_grad_ref, up_grad_ref, place_ref, gate_ref, up_ref, out_refs, back_ref, columns)


def rest_kernel(sources, columns, kept_ref, gate_grad_ref, up_grad_ref, place_ref, gate_ref, up_ref, *refs):
    row_piece(
        kept_ref, gate_grad_ref, up_grad_ref, place_ref, gate_ref, up_ref, refs[:sources], refs[sources], columns
    )


def hold_kernel(index, value_ref, *refs):
    refs[-1][...] = value_ref[index]


def turn_kernel(count, *refs):
    e = pl.program_id(0)
    refs = refs[3:]
    for from_ref, to_ref in zip(refs[:count], refs[count:]):
        to_ref[e] = from_ref[0].T
    refs[-1][...] = jnp.zeros_like(refs[-1])


def turn_into_kernel(from_ref, after_ref, held_ref, to_ref, done_ref):
    to_ref[pl.program_id(0)] = from_ref[0].T
    done_ref[...] = jnp.zeros_like(done_ref)


def first_kernel(saved_ref, grad_ref, routes_from, weights_from, out_ref, grad_out_ref, routes_ref, weights_ref, sems):
    tokens = saved_ref.shape[1]
    copies = [
        pltpu.make_async_copy(routes_from, routes_ref, sems.at[0]),
        pltpu.make_async_copy(weights_from, weights_ref, sems.at[1]),
        pltpu.make_async_copy(saved_ref.at[0], out_ref.at[:tokens], sems.at[2]),
        pltpu.make_async_copy(grad_ref, grad_out_ref, sems.at[3]),
    ]
    for copy in copies:
        copy.start()
    copies[0].wait()
    copies[1].wait()
    rows = []
    for step in range(routes_ref.shape[0]):
        weight = weights_ref[step]
        high = weight.astype(BF16).astype(F32)
        middle = (weight - high).astype(BF16).astype(F32)
        for part in (routes_ref[step].astype(F32), high, middle, weight - high - middle):
            rows.append(jnp.concatenate([part[k : k + 1] for k in range(part.shape[0])], axis=1))
    out_ref[tokens:] = jnp.concatenate(rows, axis=0).astype(BF16)
    for copy in copies[2:]:
        copy.wait()


VMEM = pl.BlockSpec(memory_space=pltpu.VMEM)
MIB = 1024 * 1024
SMALL = pl.CostEstimate(flops=0, bytes_accessed=1024, transcendentals=0)
DONE = pltpu.VMEM((8, 128), F32)


def near(*values):
    return [pltpu.with_memory_space_constraint(v, pltpu.VMEM) for v in values]


def one(shape):
    return pl.BlockSpec((1,) + shape[1:], lambda e: (e,) + (0,) * (len(shape) - 1))


def turned(who, after, *weights):
    local = weights[0].shape[0]
    shapes = [(local, w.shape[2], w.shape[1]) for w in weights]
    return pl.pallas_call(
        functools.partial(turn_kernel, len(weights) - 1),
        grid=(local,),
        in_specs=[pl.BlockSpec(memory_space=pltpu.SMEM)] * 2 + [VMEM] + [one(w.shape) for w in weights[:-1]],
        out_specs=(VMEM,) * (len(weights) + 1),
        out_shape=(*[pltpu.VMEM(shape, BF16) for shape in shapes], DONE),
        compiler_params=pltpu.CompilerParams(vmem_limit_bytes=10 * MIB),
        cost_estimate=SMALL,
        name="turn",
    )(*who, *near(after), *[pltpu.with_memory_space_constraint(w, pltpu.HBM) for w in weights[:-1]])


def turned_into(place, after, weight):
    return pl.pallas_call(
        turn_into_kernel,
        grid=(weight.shape[0],),
        in_specs=[one(weight.shape), VMEM, VMEM],
        out_specs=(VMEM, VMEM),
        out_shape=(pltpu.VMEM(place.shape, BF16), DONE),
        input_output_aliases={2: 0},
        compiler_params=pltpu.CompilerParams(vmem_limit_bytes=6 * MIB),
        cost_estimate=SMALL,
        name="turn_into",
    )(pltpu.with_memory_space_constraint(weight, pltpu.HBM), *near(after, place))


def first_blocks(saved, grad, routes, weights):
    steps, tokens, width = saved.shape
    return pl.pallas_call(
        first_kernel,
        in_specs=[pl.BlockSpec(memory_space=pl.ANY)] * 4,
        out_specs=(VMEM,) * 2,
        out_shape=(pltpu.VMEM((tokens + 4 * steps, width), BF16), pltpu.VMEM(grad.shape, BF16)),
        scratch_shapes=[
            pltpu.VMEM(routes.shape, routes.dtype),
            pltpu.VMEM(weights.shape, weights.dtype),
            pltpu.SemaphoreType.DMA((4,)),
        ],
        compiler_params=pltpu.CompilerParams(vmem_limit_bytes=2 * MIB),
        cost_estimate=SMALL,
        name="first",
    )(*[pltpu.with_memory_space_constraint(v, pltpu.HBM) for v in (saved, grad, routes, weights)])


def choose_kernel(odd_ref, done_ref, left_ref, right_ref, out_ref):
    @pl.when(odd_ref[0] == 1)
    def _():
        out_ref[...] = right_ref[...]

    @pl.when(odd_ref[0] == 0)
    def _():
        out_ref[...] = left_ref[...]


def chosen(who, done, left, right):
    done = left if done is who[1] else done
    return pl.pallas_call(
        choose_kernel,
        in_specs=[pl.BlockSpec(memory_space=pltpu.SMEM)] + [VMEM] * 3,
        out_specs=VMEM,
        out_shape=pltpu.VMEM(left.shape, left.dtype),
        compiler_params=pltpu.CompilerParams(vmem_limit_bytes=2 * MIB),
        cost_estimate=SMALL,
        name="choose",
    )(who[1], *near(done, left, right))


def join_kernel(odd_ref, far_ref, left_ref, right_ref, *refs):
    to_left_ref, to_right_ref = refs[-2:]
    far = far_ref[...].astype(F32)

    @pl.when(odd_ref[0] == 1)
    def _():
        to_left_ref[...] = left_ref[...]
        to_right_ref[...] = (right_ref[...].astype(F32) + far).astype(BF16)

    @pl.when(odd_ref[0] == 0)
    def _():
        to_left_ref[...] = (left_ref[...].astype(F32) + far).astype(BF16)
        to_right_ref[...] = right_ref[...]


def joined(who, far, left, right, beside):
    return pl.pallas_call(
        join_kernel,
        in_specs=[pl.BlockSpec(memory_space=pltpu.SMEM)] + [VMEM] * (3 + len(beside)),
        out_specs=(VMEM,) * 2,
        out_shape=(pltpu.VMEM(left.shape, left.dtype),) * 2,
        compiler_params=pltpu.CompilerParams(vmem_limit_bytes=2 * MIB),
        cost_estimate=SMALL,
        name="join",
    )(who[1], *near(far, left, right, *beside))


def held(value, index, *after):
    return pl.pallas_call(
        functools.partial(hold_kernel, index),
        in_specs=[VMEM] * (1 + len(after)),
        out_specs=VMEM,
        out_shape=pltpu.VMEM(value.shape[1:], value.dtype),
        compiler_params=pltpu.CompilerParams(vmem_limit_bytes=2 * MIB),
        cost_estimate=SMALL,
        name="hold",
    )(*near(value, *after))


def forward(step, who, tokens, xs, metas, gate, up):
    sources, local = len(xs), gate.shape[0]
    width = xs[0].shape[1]
    hidden = gate.shape[1]
    rows = sources * MOST
    arrays = (*xs, *metas, gate, up) if step else (*xs, gate, up)
    return pl.pallas_call(
        functools.partial(forward_kernel, sources, local, tokens, step),
        in_specs=[pl.BlockSpec(memory_space=pltpu.SMEM)] + [VMEM] * len(arrays),
        out_specs=(VMEM,) * 5,
        out_shape=(
            pltpu.VMEM((local, rows, hidden), F32),
            pltpu.VMEM((local, rows, hidden), F32),
            pltpu.VMEM((sources // 2, local * PAIR, 2 * tokens), BF16),
            pltpu.VMEM((sources // 2, 2 * tokens, local * PAIR), BF16),
            DONE,
        ),
        scratch_shapes=[
            pltpu.VMEM((local, rows, width), BF16),
            pltpu.VMEM((local, rows, 1), F32),
        ],
        compiler_params=pltpu.CompilerParams(vmem_limit_bytes=9 * MIB),
        cost_estimate=SMALL,
        name="forward",
    )(who[0], *near(*arrays))


def backward(gs, a, b, pick, place, gate, up, down, kept_type):
    sources, pieces, local = len(gs), len(gs[0]), gate.shape[0]
    tokens = gs[0][0].shape[0]
    hidden, width = gate.shape[1:]
    rows = sources * MOST
    half = width // 2
    types = [kept_type] + [BF16] * (sources - 1)
    outs = tuple(pltpu.VMEM((tokens, half), t) for t in types)
    factor = pltpu.VMEM((local, rows, hidden), BF16)
    back = pltpu.VMEM((sources // 2, local, PAIR, half), BF16)
    *first, gate_grad, up_grad = pl.pallas_call(
        functools.partial(backward_kernel, sources, pieces, slice(0, half)),
        in_specs=[VMEM] * (sources * pieces + 7),
        out_specs=(VMEM,) * (sources + 2),
        out_shape=outs + (factor, factor),
        scratch_shapes=[pltpu.VMEM((local, rows, width), BF16), back],
        compiler_params=pltpu.CompilerParams(vmem_limit_bytes=11 * MIB),
        cost_estimate=SMALL,
        name="backward",
    )(*near(*[g for block in gs for g in block], a, b, pick, place, gate, up, down))
    rest = pl.pallas_call(
        functools.partial(rest_kernel, sources, slice(half, width)),
        in_specs=[VMEM] * 6,
        out_specs=(VMEM,) * sources,
        out_shape=outs,
        scratch_shapes=[back],
        compiler_params=pltpu.CompilerParams(vmem_limit_bytes=6 * MIB),
        cost_estimate=SMALL,
        name="rest",
    )(*near(gs[0][-1], gate_grad, up_grad, place, gate, up))
    return first, rest


def moved(value, by):
    count = lax.axis_size("expert")
    return lax.ppermute(value, "expert", [(i, (i + by) % count) for i in range(count)])


def swapped(value):
    return lax.ppermute(value, "expert", [(i, i ^ 1) for i in range(lax.axis_size("expert"))])


def moved_back(value, by):
    sections, count = lax.axis_size("section"), lax.axis_size("expert")
    pairs = [
        (s * count + i, ((s - 1) % sections) * count + (i + by) % count)
        for s in range(sections)
        for i in range(count)
    ]
    return lax.ppermute(value, ("section", "expert"), pairs)


def gathered_near(value):
    count = lax.axis_size("expert")
    if count != 4:
        return [value] + [moved(value, k) for k in range(1, count)]
    return [value, moved(value, 1), None, moved(value, -1)]


def gathered_far(who, blocks, done):
    if blocks[2] is not None:
        return blocks, None
    value, left, _, right = blocks
    passed = chosen(who, done, left, right)
    return [value, left, swapped(passed), right], passed


def joined_parts(who, parts, beside):
    if lax.axis_size("expert") != 4:
        return [(parts[k], -k) for k in range(1, len(parts))]
    _, left, far, right = parts
    to_left, to_right = joined(who, swapped(far), left, right, beside)
    return [(to_left, -1), (to_right, 1)]


def sum_kernel(count, *refs):
    total = refs[0][...].astype(F32)
    for ref in refs[1:count]:
        total = total + ref[...].astype(F32)
    refs[-1][...] = total.astype(BF16)


def scattered(own, sent, last, after):
    move = moved if last else moved_back
    terms = [own if last else move(own, 0)] + [move(part, by) for part, by in sent]
    return pl.pallas_call(
        functools.partial(sum_kernel, len(terms)),
        in_specs=[VMEM] * (len(terms) + len(after)),
        out_specs=VMEM,
        out_shape=pltpu.VMEM(own.shape, BF16),
        compiler_params=pltpu.CompilerParams(vmem_limit_bytes=2 * MIB),
        cost_estimate=SMALL,
        name="sum",
    )(*near(*terms, *after))


def shards(grad_out, saved_inputs, routes, gate_weights, w_gate, w_up, w_down):
    gate, up, down = w_gate[0], w_up[0], w_down[0]
    local = gate.shape[0]
    tokens = grad_out.shape[1]
    steps = routes.shape[1]
    ringed = lax.axis_size("expert") == 4
    place = lax.axis_index("expert").astype(jnp.int32)
    who = ((place * local).reshape(1), (place % 2).reshape(1))
    first, grad = first_blocks(
        saved_inputs[0], grad_out[0], routes[0].transpose(0, 2, 1), gate_weights[0].transpose(0, 2, 1)
    )
    xs = gathered_near(first)
    gs = gathered_near(grad)
    *back, done = turned(who, first, gate, up, down)
    xs, passed = gathered_far(who, xs, done)
    metas = xs
    back[2], done = turned_into(back[2], passed if ringed else first, down)
    gs, passed = gathered_far(who, gs, done)
    gs = [[g] for g in gs]
    for step in range(steps):
        last = step + 1 == steps
        *factors, done = forward(step, who, tokens, xs, metas, back[0], back[1])
        if step:
            gs = [list(block) for block in zip(*[gathered_far(who, g, done)[0] for g in gs])]
        beside = ()
        if not last:
            following = held(saved_inputs[0], step + 1, passed) if ringed else saved_inputs[0, step + 1]
            xs = gathered_near(following)
            beside = xs[1::2] if ringed else ()
        halves = backward(gs, *factors, *back, F32 if last else BF16)
        sent = [joined_parts(who, parts, beside) for parts in halves]
        grads = []
        for parts, pairs in zip(halves, sent):
            grads.append(scattered(parts[0], pairs, last, grads))
        if not last:
            xs, _ = gathered_far(who, xs, done)
            gs = [gathered_near(grad) for grad in grads]
    return jnp.concatenate(grads, axis=1)[None]


def solution(mesh):
    placed = (
        P("section", "expert", None),
        P("section", None, "expert", None),
        P("section", None, "expert", None),
        P("section", None, "expert", None),
        P("section", "expert", None, None),
        P("section", "expert", None, None),
        P("section", "expert", None, None),
    )
    return jax.shard_map(
        shards, mesh=mesh, in_specs=placed, out_specs=P("section", "expert", None), check_vma=False
    )
```

```python
import functools

import jax
import jax.numpy as jnp
from jax import lax
from jax.experimental import pallas as pl
from jax.experimental.pallas import tpu as pltpu
from jax.sharding import PartitionSpec as P

MOST = 40
PAIR = 2 * MOST
CUTS = (512, 512)
F32 = jnp.float32
BF16 = jnp.bfloat16


def dot(a, b, dims):
    return lax.dot_general(a, b, (dims, ((), ())), preferred_element_type=F32)


def expanded(local):
    slot = lax.broadcasted_iota(jnp.int32, (local, local * PAIR), 1)
    first = lax.broadcasted_iota(jnp.int32, (local, local * PAIR), 0) * PAIR
    return jnp.where((slot >= first) & (slot < first + PAIR), 1.0, 0.0).astype(BF16)


def forward_kernel(sources, local, tokens, step, base_ref, *refs):
    x_refs, refs = refs[:sources], refs[sources:]
    if step:
        meta_refs, refs = refs[:sources], refs[sources:]
    else:
        meta_refs = x_refs
    gate_ref, up_ref, a_ref, b_ref, pick_ref, place_ref, done_ref, rows_ref, weight_ref = refs
    top = x_refs[0].shape[1] // tokens

    mine = lax.broadcasted_iota(jnp.int32, (local, tokens), 0).astype(F32) + base_ref[0].astype(F32)
    before = (
        lax.broadcasted_iota(jnp.int32, (tokens, tokens), 0)
        < lax.broadcasted_iota(jnp.int32, (tokens, tokens), 1)
    )
    before = jnp.where(before, 1.0, 0.0).astype(BF16)
    table = expanded(local)
    for pair in range(sources // 2):
        targets, weights = [], []
        for half in range(2):
            meta = meta_refs[2 * pair + half][tokens:, :].astype(F32)[4 * step : 4 * step + 4]
            weights_of = meta[1:2] + meta[2:3] + meta[3:4]
            named = jnp.zeros((local, tokens), F32)
            weight = jnp.zeros((local, tokens), F32)
            for k in range(top):
                lanes = slice(k * tokens, (k + 1) * tokens)
                same = meta[0:1, lanes] == mine
                named = jnp.where(same, 1.0, named)
                weight = jnp.where(same, weights_of[:, lanes], weight)
            position = dot(named.astype(BF16), before, ((1,), (0,)))
            targets.append(jnp.where(named > 0.5, position + half * MOST, -1.0))
            weights.append(weight)
        target = jnp.concatenate(targets, axis=1).astype(BF16)
        weight = jnp.concatenate(weights, axis=1)
        spread = dot(table, target, ((0,), (0,)))
        slot = lax.broadcasted_iota(jnp.int32, spread.shape, 0) % PAIR
        picked = spread == slot.astype(F32)
        pick_ref[pair] = jnp.where(picked, 1.0, 0.0).astype(BF16)
        spread_t = dot(target, table, ((0,), (0,)))
        slot_t = lax.broadcasted_iota(jnp.int32, spread_t.shape, 1) % PAIR
        place_ref[pair] = jnp.where(spread_t == slot_t.astype(F32), 1.0, 0.0).astype(BF16)
        for e in range(local):
            block = jnp.where(picked[e * PAIR : (e + 1) * PAIR], weight[e : e + 1], 0.0)
            weight_ref[e, pair * PAIR : (pair + 1) * PAIR, :] = jnp.sum(block, axis=1, keepdims=True)
    pick_rows(x_refs, tokens, pick_ref, rows_ref)
    for e in range(local):
        rows = rows_ref[e]
        gate = dot(rows, gate_ref[e], ((1,), (1,)))
        up = dot(rows, up_ref[e], ((1,), (1,)))
        sig = 1.0 / (1.0 + jnp.exp(-gate))
        scaled = sig * weight_ref[e]
        a_ref[e] = up * scaled * (1.0 + gate * (1.0 - sig))
        b_ref[e] = gate * scaled
    done_ref[...] = jnp.zeros_like(done_ref)


def pick_rows(source_refs, tokens, pick_ref, rows_ref):
    local, width = rows_ref.shape[0], rows_ref.shape[2]
    for pair in range(len(source_refs) // 2):
        source = jnp.concatenate([ref[:tokens] for ref in source_refs[2 * pair : 2 * pair + 2]], axis=0)
        for n in range(0, width, 256):
            stop = min(n + 256, width)
            rows = dot(pick_ref[pair], source[:, n:stop], ((1,), (0,))).astype(BF16)
            rows_ref[:, pair * PAIR : (pair + 1) * PAIR, n:stop] = rows.reshape(local, PAIR, stop - n)


def pick_pieces(sources, pieces, piece_refs, pick_ref, rows_ref):
    start = 0
    for piece in range(pieces):
        refs = [piece_refs[k * pieces + piece] for k in range(sources)]
        tokens, width = refs[0].shape
        pick_rows(refs, tokens, pick_ref, rows_ref.at[:, :, start : start + width])
        start += width


def columns_of(refs, start, stop):
    parts, first = [], 0
    for ref in refs:
        last = first + ref.shape[1]
        if first < stop and start < last:
            parts.append(ref[:, max(start - first, 0) : min(stop, last) - first])
        first = last
    return jnp.concatenate(parts, axis=1)


def row_piece(kept_refs, gate_grad_ref, up_grad_ref, place_ref, gate_ref, up_ref, out_refs, back_ref, columns):
    local = gate_ref.shape[0]
    pairs, double = place_ref.shape[0], place_ref.shape[1]
    tokens = double // 2
    for e in range(local):
        row = dot(gate_grad_ref[e], gate_ref[e, :, columns], ((1,), (0,)))
        row = (row + dot(up_grad_ref[e], up_ref[e, :, columns], ((1,), (0,)))).astype(BF16)
        for pair in range(pairs):
            back_ref[pair, e] = row[pair * PAIR : (pair + 1) * PAIR]
    width = columns.stop - columns.start
    for pair in range(pairs):
        for n in range(0, width, 256):
            stop = min(n + 256, width)
            rows = back_ref[pair, :, :, n:stop].reshape(local * PAIR, stop - n)
            total = dot(place_ref[pair], rows, ((1,), (0,)))
            for half in range(2):
                out = out_refs[2 * pair + half]
                part = total[half * tokens : (half + 1) * tokens]
                if pair == 0 and half == 0:
                    part = part + columns_of(kept_refs, columns.start + n, columns.start + stop).astype(F32)
                out[:, n:stop] = part.astype(out.dtype)


def backward_kernel(sources, pieces, columns, *refs):
    g_refs, refs = refs[: sources * pieces], refs[sources * pieces :]
    a_ref, b_ref, pick_ref, place_ref, gate_ref, up_ref, down_ref = refs[:7]
    out_refs, refs = refs[7 : 7 + sources], refs[7 + sources :]
    gate_grad_ref, up_grad_ref, rows_ref, back_ref = refs
    pick_pieces(sources, pieces, g_refs, pick_ref, rows_ref)
    for e in range(rows_ref.shape[0]):
        hidden = dot(rows_ref[e], down_ref[e], ((1,), (0,)))
        gate_grad_ref[e] = (hidden * a_ref[e]).astype(BF16)
        up_grad_ref[e] = (hidden * b_ref[e]).astype(BF16)
    row_piece(g_refs[:pieces], gate_grad_ref, up_grad_ref, place_ref, gate_ref, up_ref, out_refs, back_ref, columns)


def rest_kernel(sources, pieces, columns, *refs):
    kept_refs, refs = refs[:pieces], refs[pieces:]
    gate_grad_ref, up_grad_ref, place_ref, gate_ref, up_ref, *refs = refs
    row_piece(
        kept_refs, gate_grad_ref, up_grad_ref, place_ref, gate_ref, up_ref, refs[:sources], refs[sources], columns
    )


def hold_kernel(index, value_ref, *refs):
    refs[-1][...] = value_ref[index]


def turn_kernel(count, *refs):
    e = pl.program_id(0)
    refs = refs[3:]
    for from_ref, to_ref in zip(refs[:count], refs[count:]):
        to_ref[e] = from_ref[0].T
    refs[-1][...] = jnp.zeros_like(refs[-1])


def turn_into_kernel(from_ref, after_ref, held_ref, to_ref, done_ref):
    to_ref[pl.program_id(0)] = from_ref[0].T
    done_ref[...] = jnp.zeros_like(done_ref)


def first_kernel(saved_ref, grad_ref, routes_from, weights_from, out_ref, grad_out_ref, routes_ref, weights_ref, sems):
    tokens = saved_ref.shape[1]
    copies = [
        pltpu.make_async_copy(routes_from, routes_ref, sems.at[0]),
        pltpu.make_async_copy(weights_from, weights_ref, sems.at[1]),
        pltpu.make_async_copy(saved_ref.at[0], out_ref.at[:tokens], sems.at[2]),
        pltpu.make_async_copy(grad_ref, grad_out_ref, sems.at[3]),
    ]
    for copy in copies:
        copy.start()
    copies[0].wait()
    copies[1].wait()
    rows = []
    for step in range(routes_ref.shape[0]):
        weight = weights_ref[step]
        high = weight.astype(BF16).astype(F32)
        middle = (weight - high).astype(BF16).astype(F32)
        for part in (routes_ref[step].astype(F32), high, middle, weight - high - middle):
            rows.append(jnp.concatenate([part[k : k + 1] for k in range(part.shape[0])], axis=1))
    out_ref[tokens:] = jnp.concatenate(rows, axis=0).astype(BF16)
    for copy in copies[2:]:
        copy.wait()


VMEM = pl.BlockSpec(memory_space=pltpu.VMEM)
MIB = 1024 * 1024
SMALL = pl.CostEstimate(flops=0, bytes_accessed=1024, transcendentals=0)
DONE = pltpu.VMEM((8, 128), F32)


def near(*values):
    return [pltpu.with_memory_space_constraint(v, pltpu.VMEM) for v in values]


def one(shape):
    return pl.BlockSpec((1,) + shape[1:], lambda e: (e,) + (0,) * (len(shape) - 1))


def turned(who, after, *weights):
    local = weights[0].shape[0]
    shapes = [(local, w.shape[2], w.shape[1]) for w in weights]
    return pl.pallas_call(
        functools.partial(turn_kernel, len(weights) - 1),
        grid=(local,),
        in_specs=[pl.BlockSpec(memory_space=pltpu.SMEM)] * 2 + [VMEM] + [one(w.shape) for w in weights[:-1]],
        out_specs=(VMEM,) * (len(weights) + 1),
        out_shape=(*[pltpu.VMEM(shape, BF16) for shape in shapes], DONE),
        compiler_params=pltpu.CompilerParams(vmem_limit_bytes=10 * MIB),
        cost_estimate=SMALL,
        name="turn",
    )(*who, *near(after), *[pltpu.with_memory_space_constraint(w, pltpu.HBM) for w in weights[:-1]])


def turned_into(place, after, weight):
    return pl.pallas_call(
        turn_into_kernel,
        grid=(weight.shape[0],),
        in_specs=[one(weight.shape), VMEM, VMEM],
        out_specs=(VMEM, VMEM),
        out_shape=(pltpu.VMEM(place.shape, BF16), DONE),
        input_output_aliases={2: 0},
        compiler_params=pltpu.CompilerParams(vmem_limit_bytes=6 * MIB),
        cost_estimate=SMALL,
        name="turn_into",
    )(pltpu.with_memory_space_constraint(weight, pltpu.HBM), *near(after, place))


def first_blocks(saved, grad, routes, weights):
    steps, tokens, width = saved.shape
    return pl.pallas_call(
        first_kernel,
        in_specs=[pl.BlockSpec(memory_space=pl.ANY)] * 4,
        out_specs=(VMEM,) * 2,
        out_shape=(pltpu.VMEM((tokens + 4 * steps, width), BF16), pltpu.VMEM(grad.shape, BF16)),
        scratch_shapes=[
            pltpu.VMEM(routes.shape, routes.dtype),
            pltpu.VMEM(weights.shape, weights.dtype),
            pltpu.SemaphoreType.DMA((4,)),
        ],
        compiler_params=pltpu.CompilerParams(vmem_limit_bytes=2 * MIB),
        cost_estimate=SMALL,
        name="first",
    )(*[pltpu.with_memory_space_constraint(v, pltpu.HBM) for v in (saved, grad, routes, weights)])


def choose_kernel(odd_ref, done_ref, left_ref, right_ref, out_ref):
    @pl.when(odd_ref[0] == 1)
    def _():
        out_ref[...] = right_ref[...]

    @pl.when(odd_ref[0] == 0)
    def _():
        out_ref[...] = left_ref[...]


def chosen(who, done, left, right):
    done = left if done is who[1] else done
    return pl.pallas_call(
        choose_kernel,
        in_specs=[pl.BlockSpec(memory_space=pltpu.SMEM)] + [VMEM] * 3,
        out_specs=VMEM,
        out_shape=pltpu.VMEM(left.shape, left.dtype),
        compiler_params=pltpu.CompilerParams(vmem_limit_bytes=2 * MIB),
        cost_estimate=SMALL,
        name="choose",
    )(who[1], *near(done, left, right))


def join_kernel(odd_ref, far_ref, left_ref, right_ref, *refs):
    to_left_ref, to_right_ref = refs[-2:]
    far = far_ref[...].astype(F32)

    @pl.when(odd_ref[0] == 1)
    def _():
        to_left_ref[...] = left_ref[...]
        to_right_ref[...] = (right_ref[...].astype(F32) + far).astype(BF16)

    @pl.when(odd_ref[0] == 0)
    def _():
        to_left_ref[...] = (left_ref[...].astype(F32) + far).astype(BF16)
        to_right_ref[...] = right_ref[...]


def joined(who, far, left, right, beside):
    return pl.pallas_call(
        join_kernel,
        in_specs=[pl.BlockSpec(memory_space=pltpu.SMEM)] + [VMEM] * (3 + len(beside)),
        out_specs=(VMEM,) * 2,
        out_shape=(pltpu.VMEM(left.shape, left.dtype),) * 2,
        compiler_params=pltpu.CompilerParams(vmem_limit_bytes=2 * MIB),
        cost_estimate=SMALL,
        name="join",
    )(who[1], *near(far, left, right, *beside))


def held(value, index, *after):
    return pl.pallas_call(
        functools.partial(hold_kernel, index),
        in_specs=[VMEM] * (1 + len(after)),
        out_specs=VMEM,
        out_shape=pltpu.VMEM(value.shape[1:], value.dtype),
        compiler_params=pltpu.CompilerParams(vmem_limit_bytes=2 * MIB),
        cost_estimate=SMALL,
        name="hold",
    )(*near(value, *after))


def forward(step, who, tokens, xs, metas, gate, up):
    sources, local = len(xs), gate.shape[0]
    width = xs[0].shape[1]
    hidden = gate.shape[1]
    rows = sources * MOST
    arrays = (*xs, *metas, gate, up) if step else (*xs, gate, up)
    return pl.pallas_call(
        functools.partial(forward_kernel, sources, local, tokens, step),
        in_specs=[pl.BlockSpec(memory_space=pltpu.SMEM)] + [VMEM] * len(arrays),
        out_specs=(VMEM,) * 5,
        out_shape=(
            pltpu.VMEM((local, rows, hidden), F32),
            pltpu.VMEM((local, rows, hidden), F32),
            pltpu.VMEM((sources // 2, local * PAIR, 2 * tokens), BF16),
            pltpu.VMEM((sources // 2, 2 * tokens, local * PAIR), BF16),
            DONE,
        ),
        scratch_shapes=[
            pltpu.VMEM((local, rows, width), BF16),
            pltpu.VMEM((local, rows, 1), F32),
        ],
        compiler_params=pltpu.CompilerParams(vmem_limit_bytes=9 * MIB),
        cost_estimate=SMALL,
        name="forward",
    )(who[0], *near(*arrays))


def backward(cut, kept_type, gs, a, b, pick, place, gate, up, down):
    sources, pieces, local = len(gs), len(gs[0]), gate.shape[0]
    tokens = gs[0][0].shape[0]
    hidden, width = gate.shape[1:]
    rows = sources * MOST
    types = [kept_type] + [BF16] * (sources - 1)
    outs = [tuple(pltpu.VMEM((tokens, w), t) for t in types) for w in (cut, width - cut)]
    factor = pltpu.VMEM((local, rows, hidden), BF16)
    backs = [pltpu.VMEM((sources // 2, local, PAIR, w), BF16) for w in (cut, width - cut)]
    *first, gate_grad, up_grad = pl.pallas_call(
        functools.partial(backward_kernel, sources, pieces, slice(0, cut)),
        in_specs=[VMEM] * (sources * pieces + 7),
        out_specs=(VMEM,) * (sources + 2),
        out_shape=outs[0] + (factor, factor),
        scratch_shapes=[pltpu.VMEM((local, rows, width), BF16), backs[0]],
        compiler_params=pltpu.CompilerParams(vmem_limit_bytes=11 * MIB),
        cost_estimate=SMALL,
        name="backward",
    )(*near(*[g for block in gs for g in block], a, b, pick, place, gate, up, down))
    rest = pl.pallas_call(
        functools.partial(rest_kernel, sources, pieces, slice(cut, width)),
        in_specs=[VMEM] * (pieces + 5),
        out_specs=(VMEM,) * sources,
        out_shape=outs[1],
        scratch_shapes=[backs[1]],
        compiler_params=pltpu.CompilerParams(vmem_limit_bytes=7 * MIB),
        cost_estimate=SMALL,
        name="rest",
    )(*near(*gs[0], gate_grad, up_grad, place, gate, up))
    return first, rest


def moved(value, by):
    count = lax.axis_size("expert")
    return lax.ppermute(value, "expert", [(i, (i + by) % count) for i in range(count)])


def swapped(value):
    return lax.ppermute(value, "expert", [(i, i ^ 1) for i in range(lax.axis_size("expert"))])


def moved_back(value, by):
    sections, count = lax.axis_size("section"), lax.axis_size("expert")
    pairs = [
        (s * count + i, ((s - 1) % sections) * count + (i + by) % count)
        for s in range(sections)
        for i in range(count)
    ]
    return lax.ppermute(value, ("section", "expert"), pairs)


def gathered_near(value):
    count = lax.axis_size("expert")
    if count != 4:
        return [value] + [moved(value, k) for k in range(1, count)]
    return [value, moved(value, 1), None, moved(value, -1)]


def gathered_far(who, blocks, done):
    if blocks[2] is not None:
        return blocks, None
    value, left, _, right = blocks
    passed = chosen(who, done, left, right)
    return [value, left, swapped(passed), right], passed


def joined_parts(who, parts, beside):
    if lax.axis_size("expert") != 4:
        return [(parts[k], -k) for k in range(1, len(parts))]
    _, left, far, right = parts
    to_left, to_right = joined(who, swapped(far), left, right, beside)
    return [(to_left, -1), (to_right, 1)]


def sum_kernel(count, *refs):
    total = refs[0][...].astype(F32)
    for ref in refs[1:count]:
        total = total + ref[...].astype(F32)
    refs[-1][...] = total.astype(BF16)


def scattered(own, sent, last, after):
    move = moved if last else moved_back
    terms = [own] + [move(part, by) for part, by in sent]
    return pl.pallas_call(
        functools.partial(sum_kernel, len(terms)),
        in_specs=[VMEM] * (len(terms) + len(after)),
        out_specs=VMEM,
        out_shape=pltpu.VMEM(own.shape, BF16),
        compiler_params=pltpu.CompilerParams(vmem_limit_bytes=2 * MIB),
        cost_estimate=SMALL,
        name="sum",
    )(*near(*terms, *after))


def shards(grad_out, saved_inputs, routes, gate_weights, w_gate, w_up, w_down):
    gate, up, down = w_gate[0], w_up[0], w_down[0]
    local = gate.shape[0]
    tokens = grad_out.shape[1]
    steps = routes.shape[1]
    ringed = lax.axis_size("expert") == 4
    place = lax.axis_index("expert").astype(jnp.int32)
    who = ((place * local).reshape(1), (place % 2).reshape(1))
    first, grad = first_blocks(
        saved_inputs[0], grad_out[0], routes[0].transpose(0, 2, 1), gate_weights[0].transpose(0, 2, 1)
    )
    xs = gathered_near(first)
    gs = gathered_near(grad)
    *back, done = turned(who, first, gate, up, down)
    xs, passed = gathered_far(who, xs, done)
    metas = xs
    back[2], done = turned_into(back[2], passed if ringed else first, down)
    gs, passed = gathered_far(who, gs, done)
    gs = [[g] for g in gs]
    for step in range(steps):
        last = step + 1 == steps
        *factors, done = forward(step, who, tokens, xs, metas, back[0], back[1])
        if step:
            gs = [list(block) for block in zip(*[gathered_far(who, g, done)[0] for g in gs])]
        beside = ()
        if not last:
            following = held(saved_inputs[0], step + 1, passed) if ringed else saved_inputs[0, step + 1]
            xs = gathered_near(following)
            beside = xs[1::2] if ringed else ()
        halves = backward(CUTS[last], F32 if last else BF16, gs, *factors, *back)
        owns = [parts[0] if last else moved_back(parts[0], 0) for parts in halves]
        sent = []
        for own, parts in zip(owns, halves):
            sent.append(joined_parts(who, parts, (*beside, own)))
        grads = []
        for own, pairs in zip(owns, sent):
            grads.append(scattered(own, pairs, last, grads))
        if not last:
            xs, _ = gathered_far(who, xs, done)
            gs = [gathered_near(grad) for grad in grads]
    return jnp.concatenate(grads, axis=1)[None]


def solution(mesh):
    placed = (
        P("section", "expert", None),
        P("section", None, "expert", None),
        P("section", None, "expert", None),
        P("section", None, "expert", None),
        P("section", "expert", None, None),
        P("section", "expert", None, None),
        P("section", "expert", None, None),
    )
    return jax.shard_map(
        shards, mesh=mesh, in_specs=placed, out_specs=P("section", "expert", None), check_vma=False
    )
```

```python
import functools

import jax
import jax.numpy as jnp
from jax import lax
from jax.experimental import pallas as pl
from jax.experimental.pallas import tpu as pltpu
from jax.sharding import PartitionSpec as P

MOST = 40
PAIR = 2 * MOST
CUTS = (512, 512)
F32 = jnp.float32
BF16 = jnp.bfloat16


def dot(a, b, dims):
    return lax.dot_general(a, b, (dims, ((), ())), preferred_element_type=F32)


def expanded(local):
    slot = lax.broadcasted_iota(jnp.int32, (local, local * PAIR), 1)
    first = lax.broadcasted_iota(jnp.int32, (local, local * PAIR), 0) * PAIR
    return jnp.where((slot >= first) & (slot < first + PAIR), 1.0, 0.0).astype(BF16)


def forward_kernel(sources, local, tokens, step, base_ref, *refs):
    x_refs, refs = refs[:sources], refs[sources:]
    if step:
        meta_refs, refs = refs[:sources], refs[sources:]
    else:
        meta_refs = x_refs
    gate_ref, up_ref, a_ref, b_ref, pick_ref, place_ref, done_ref, rows_ref, weight_ref = refs
    top = x_refs[0].shape[1] // tokens

    mine = lax.broadcasted_iota(jnp.int32, (local, tokens), 0).astype(F32) + base_ref[0].astype(F32)
    before = (
        lax.broadcasted_iota(jnp.int32, (tokens, tokens), 0)
        < lax.broadcasted_iota(jnp.int32, (tokens, tokens), 1)
    )
    before = jnp.where(before, 1.0, 0.0).astype(BF16)
    table = expanded(local)
    for pair in range(sources // 2):
        targets, weights = [], []
        for half in range(2):
            meta = meta_refs[2 * pair + half][tokens:, :].astype(F32)[4 * step : 4 * step + 4]
            weights_of = meta[1:2] + meta[2:3] + meta[3:4]
            named = jnp.zeros((local, tokens), F32)
            weight = jnp.zeros((local, tokens), F32)
            for k in range(top):
                lanes = slice(k * tokens, (k + 1) * tokens)
                same = meta[0:1, lanes] == mine
                named = jnp.where(same, 1.0, named)
                weight = jnp.where(same, weights_of[:, lanes], weight)
            position = dot(named.astype(BF16), before, ((1,), (0,)))
            targets.append(jnp.where(named > 0.5, position + half * MOST, -1.0))
            weights.append(weight)
        target = jnp.concatenate(targets, axis=1).astype(BF16)
        weight = jnp.concatenate(weights, axis=1)
        spread = dot(table, target, ((0,), (0,)))
        slot = lax.broadcasted_iota(jnp.int32, spread.shape, 0) % PAIR
        picked = spread == slot.astype(F32)
        pick_ref[pair] = jnp.where(picked, 1.0, 0.0).astype(BF16)
        spread_t = dot(target, table, ((0,), (0,)))
        slot_t = lax.broadcasted_iota(jnp.int32, spread_t.shape, 1) % PAIR
        place_ref[pair] = jnp.where(spread_t == slot_t.astype(F32), 1.0, 0.0).astype(BF16)
        for e in range(local):
            block = jnp.where(picked[e * PAIR : (e + 1) * PAIR], weight[e : e + 1], 0.0)
            weight_ref[e, pair * PAIR : (pair + 1) * PAIR, :] = jnp.sum(block, axis=1, keepdims=True)
    pick_rows(x_refs, tokens, pick_ref, rows_ref)
    for e in range(local):
        rows = rows_ref[e]
        gate = dot(rows, gate_ref[e], ((1,), (1,)))
        up = dot(rows, up_ref[e], ((1,), (1,)))
        sig = 1.0 / (1.0 + jnp.exp(-gate))
        scaled = sig * weight_ref[e]
        a_ref[e] = up * scaled * (1.0 + gate * (1.0 - sig))
        b_ref[e] = gate * scaled
    done_ref[...] = jnp.zeros_like(done_ref)


def pick_rows(source_refs, tokens, pick_ref, rows_ref):
    local, width = rows_ref.shape[0], rows_ref.shape[2]
    for pair in range(len(source_refs) // 2):
        source = jnp.concatenate([ref[:tokens] for ref in source_refs[2 * pair : 2 * pair + 2]], axis=0)
        for n in range(0, width, 256):
            stop = min(n + 256, width)
            rows = dot(pick_ref[pair], source[:, n:stop], ((1,), (0,))).astype(BF16)
            rows_ref[:, pair * PAIR : (pair + 1) * PAIR, n:stop] = rows.reshape(local, PAIR, stop - n)


def pick_pieces(sources, pieces, piece_refs, pick_ref, rows_ref):
    start = 0
    for piece in range(pieces):
        refs = [piece_refs[k * pieces + piece] for k in range(sources)]
        tokens, width = refs[0].shape
        pick_rows(refs, tokens, pick_ref, rows_ref.at[:, :, start : start + width])
        start += width


def columns_of(refs, start, stop):
    parts, first = [], 0
    for ref in refs:
        last = first + ref.shape[1]
        if first < stop and start < last:
            parts.append(ref[:, max(start - first, 0) : min(stop, last) - first])
        first = last
    return jnp.concatenate(parts, axis=1)


def row_piece(kept_refs, gate_grad_ref, up_grad_ref, place_ref, gate_ref, up_ref, out_refs, back_ref, columns):
    local = gate_ref.shape[0]
    pairs, double = place_ref.shape[0], place_ref.shape[1]
    tokens = double // 2
    for e in range(local):
        row = dot(gate_grad_ref[e], gate_ref[e, :, columns], ((1,), (0,)))
        row = (row + dot(up_grad_ref[e], up_ref[e, :, columns], ((1,), (0,)))).astype(BF16)
        for pair in range(pairs):
            back_ref[pair, e] = row[pair * PAIR : (pair + 1) * PAIR]
    width = columns.stop - columns.start
    for pair in range(pairs):
        for n in range(0, width, 256):
            stop = min(n + 256, width)
            rows = back_ref[pair, :, :, n:stop].reshape(local * PAIR, stop - n)
            total = dot(place_ref[pair], rows, ((1,), (0,)))
            for half in range(2):
                out = out_refs[2 * pair + half]
                part = total[half * tokens : (half + 1) * tokens]
                if pair == 0 and half == 0:
                    part = part + columns_of(kept_refs, columns.start + n, columns.start + stop).astype(F32)
                out[:, n:stop] = part.astype(out.dtype)


def backward_kernel(sources, pieces, columns, *refs):
    g_refs, refs = refs[: sources * pieces], refs[sources * pieces :]
    a_ref, b_ref, pick_ref, place_ref, gate_ref, up_ref, down_ref = refs[:7]
    out_refs, refs = refs[7 : 7 + sources], refs[7 + sources :]
    gate_grad_ref, up_grad_ref, rows_ref, back_ref = refs
    pick_pieces(sources, pieces, g_refs, pick_ref, rows_ref)
    for e in range(rows_ref.shape[0]):
        hidden = dot(rows_ref[e], down_ref[e], ((1,), (0,)))
        gate_grad_ref[e] = (hidden * a_ref[e]).astype(BF16)
        up_grad_ref[e] = (hidden * b_ref[e]).astype(BF16)
    row_piece(g_refs[:pieces], gate_grad_ref, up_grad_ref, place_ref, gate_ref, up_ref, out_refs, back_ref, columns)


def rest_kernel(sources, pieces, columns, *refs):
    kept_refs, refs = refs[:pieces], refs[pieces:]
    gate_grad_ref, up_grad_ref, place_ref, gate_ref, up_ref, *refs = refs
    row_piece(
        kept_refs, gate_grad_ref, up_grad_ref, place_ref, gate_ref, up_ref, refs[:sources], refs[sources], columns
    )


def hold_kernel(index, value_ref, *refs):
    refs[-1][...] = value_ref[index]


def turn_kernel(count, *refs):
    e = pl.program_id(0)
    refs = refs[3:]
    for from_ref, to_ref in zip(refs[:count], refs[count:]):
        to_ref[e] = from_ref[0].T
    refs[-1][...] = jnp.zeros_like(refs[-1])


def turn_into_kernel(from_ref, after_ref, held_ref, to_ref, done_ref):
    to_ref[pl.program_id(0)] = from_ref[0].T
    done_ref[...] = jnp.zeros_like(done_ref)


def first_kernel(saved_ref, grad_ref, routes_from, weights_from, out_ref, grad_out_ref, routes_ref, weights_ref, sems):
    tokens = saved_ref.shape[1]
    copies = [
        pltpu.make_async_copy(routes_from, routes_ref, sems.at[0]),
        pltpu.make_async_copy(weights_from, weights_ref, sems.at[1]),
        pltpu.make_async_copy(saved_ref.at[0], out_ref.at[:tokens], sems.at[2]),
        pltpu.make_async_copy(grad_ref, grad_out_ref, sems.at[3]),
    ]
    for copy in copies:
        copy.start()
    copies[0].wait()
    copies[1].wait()
    rows = []
    for step in range(routes_ref.shape[0]):
        weight = weights_ref[step]
        high = weight.astype(BF16).astype(F32)
        middle = (weight - high).astype(BF16).astype(F32)
        for part in (routes_ref[step].astype(F32), high, middle, weight - high - middle):
            rows.append(jnp.concatenate([part[k : k + 1] for k in range(part.shape[0])], axis=1))
    out_ref[tokens:] = jnp.concatenate(rows, axis=0).astype(BF16)
    for copy in copies[2:]:
        copy.wait()


VMEM = pl.BlockSpec(memory_space=pltpu.VMEM)
MIB = 1024 * 1024
SMALL = pl.CostEstimate(flops=0, bytes_accessed=1024, transcendentals=0)
DONE = pltpu.VMEM((8, 128), F32)


def near(*values):
    return [pltpu.with_memory_space_constraint(v, pltpu.VMEM) for v in values]


def one(shape):
    return pl.BlockSpec((1,) + shape[1:], lambda e: (e,) + (0,) * (len(shape) - 1))


def turned(who, after, *weights):
    local = weights[0].shape[0]
    shapes = [(local, w.shape[2], w.shape[1]) for w in weights]
    return pl.pallas_call(
        functools.partial(turn_kernel, len(weights) - 1),
        grid=(local,),
        in_specs=[pl.BlockSpec(memory_space=pltpu.SMEM)] * 2 + [VMEM] + [one(w.shape) for w in weights[:-1]],
        out_specs=(VMEM,) * (len(weights) + 1),
        out_shape=(*[pltpu.VMEM(shape, BF16) for shape in shapes], DONE),
        compiler_params=pltpu.CompilerParams(vmem_limit_bytes=10 * MIB),
        cost_estimate=SMALL,
        name="turn",
    )(*who, *near(after), *[pltpu.with_memory_space_constraint(w, pltpu.HBM) for w in weights[:-1]])


def turned_into(place, after, weight):
    return pl.pallas_call(
        turn_into_kernel,
        grid=(weight.shape[0],),
        in_specs=[one(weight.shape), VMEM, VMEM],
        out_specs=(VMEM, VMEM),
        out_shape=(pltpu.VMEM(place.shape, BF16), DONE),
        input_output_aliases={2: 0},
        compiler_params=pltpu.CompilerParams(vmem_limit_bytes=6 * MIB),
        cost_estimate=SMALL,
        name="turn_into",
    )(pltpu.with_memory_space_constraint(weight, pltpu.HBM), *near(after, place))


def first_blocks(saved, grad, routes, weights):
    steps, tokens, width = saved.shape
    return pl.pallas_call(
        first_kernel,
        in_specs=[pl.BlockSpec(memory_space=pl.ANY)] * 4,
        out_specs=(VMEM,) * 2,
        out_shape=(pltpu.VMEM((tokens + 4 * steps, width), BF16), pltpu.VMEM(grad.shape, BF16)),
        scratch_shapes=[
            pltpu.VMEM(routes.shape, routes.dtype),
            pltpu.VMEM(weights.shape, weights.dtype),
            pltpu.SemaphoreType.DMA((4,)),
        ],
        compiler_params=pltpu.CompilerParams(vmem_limit_bytes=2 * MIB),
        cost_estimate=SMALL,
        name="first",
    )(*[pltpu.with_memory_space_constraint(v, pltpu.HBM) for v in (saved, grad, routes, weights)])


def choose_kernel(odd_ref, done_ref, left_ref, right_ref, out_ref):
    @pl.when(odd_ref[0] == 1)
    def _():
        out_ref[...] = right_ref[...]

    @pl.when(odd_ref[0] == 0)
    def _():
        out_ref[...] = left_ref[...]


def chosen(who, done, left, right):
    done = left if done is who[1] else done
    return pl.pallas_call(
        choose_kernel,
        in_specs=[pl.BlockSpec(memory_space=pltpu.SMEM)] + [VMEM] * 3,
        out_specs=VMEM,
        out_shape=pltpu.VMEM(left.shape, left.dtype),
        compiler_params=pltpu.CompilerParams(vmem_limit_bytes=2 * MIB),
        cost_estimate=SMALL,
        name="choose",
    )(who[1], *near(done, left, right))


def join_kernel(odd_ref, far_ref, left_ref, right_ref, *refs):
    to_left_ref, to_right_ref = refs[-2:]
    far = far_ref[...].astype(F32)

    @pl.when(odd_ref[0] == 1)
    def _():
        to_left_ref[...] = left_ref[...]
        to_right_ref[...] = (right_ref[...].astype(F32) + far).astype(BF16)

    @pl.when(odd_ref[0] == 0)
    def _():
        to_left_ref[...] = (left_ref[...].astype(F32) + far).astype(BF16)
        to_right_ref[...] = right_ref[...]


def joined(who, far, left, right, beside):
    return pl.pallas_call(
        join_kernel,
        in_specs=[pl.BlockSpec(memory_space=pltpu.SMEM)] + [VMEM] * (3 + len(beside)),
        out_specs=(VMEM,) * 2,
        out_shape=(pltpu.VMEM(left.shape, left.dtype),) * 2,
        compiler_params=pltpu.CompilerParams(vmem_limit_bytes=2 * MIB),
        cost_estimate=SMALL,
        name="join",
    )(who[1], *near(far, left, right, *beside))


def held(value, index, *after):
    return pl.pallas_call(
        functools.partial(hold_kernel, index),
        in_specs=[VMEM] * (1 + len(after)),
        out_specs=VMEM,
        out_shape=pltpu.VMEM(value.shape[1:], value.dtype),
        compiler_params=pltpu.CompilerParams(vmem_limit_bytes=2 * MIB),
        cost_estimate=SMALL,
        name="hold",
    )(*near(value, *after))


def forward(step, who, tokens, xs, metas, gate, up):
    sources, local = len(xs), gate.shape[0]
    width = xs[0].shape[1]
    hidden = gate.shape[1]
    rows = sources * MOST
    arrays = (*xs, *metas, gate, up) if step else (*xs, gate, up)
    return pl.pallas_call(
        functools.partial(forward_kernel, sources, local, tokens, step),
        in_specs=[pl.BlockSpec(memory_space=pltpu.SMEM)] + [VMEM] * len(arrays),
        out_specs=(VMEM,) * 5,
        out_shape=(
            pltpu.VMEM((local, rows, hidden), F32),
            pltpu.VMEM((local, rows, hidden), F32),
            pltpu.VMEM((sources // 2, local * PAIR, 2 * tokens), BF16),
            pltpu.VMEM((sources // 2, 2 * tokens, local * PAIR), BF16),
            DONE,
        ),
        scratch_shapes=[
            pltpu.VMEM((local, rows, width), BF16),
            pltpu.VMEM((local, rows, 1), F32),
        ],
        compiler_params=pltpu.CompilerParams(vmem_limit_bytes=9 * MIB),
        cost_estimate=SMALL,
        name="forward",
    )(who[0], *near(*arrays))


def backward(cut, kept_type, gs, a, b, pick, place, gate, up, down):
    sources, pieces, local = len(gs), len(gs[0]), gate.shape[0]
    tokens = gs[0][0].shape[0]
    hidden, width = gate.shape[1:]
    rows = sources * MOST
    types = [kept_type] + [BF16] * (sources - 1)
    outs = [tuple(pltpu.VMEM((tokens, w), t) for t in types) for w in (cut, width - cut)]
    factor = pltpu.VMEM((local, rows, hidden), BF16)
    backs = [pltpu.VMEM((sources // 2, local, PAIR, w), BF16) for w in (cut, width - cut)]
    *first, gate_grad, up_grad = pl.pallas_call(
        functools.partial(backward_kernel, sources, pieces, slice(0, cut)),
        in_specs=[VMEM] * (sources * pieces + 7),
        out_specs=(VMEM,) * (sources + 2),
        out_shape=outs[0] + (factor, factor),
        scratch_shapes=[pltpu.VMEM((local, rows, width), BF16), backs[0]],
        compiler_params=pltpu.CompilerParams(vmem_limit_bytes=11 * MIB),
        cost_estimate=SMALL,
        name="backward",
    )(*near(*[g for block in gs for g in block], a, b, pick, place, gate, up, down))
    rest = pl.pallas_call(
        functools.partial(rest_kernel, sources, pieces, slice(cut, width)),
        in_specs=[VMEM] * (pieces + 5),
        out_specs=(VMEM,) * sources,
        out_shape=outs[1],
        scratch_shapes=[backs[1]],
        compiler_params=pltpu.CompilerParams(vmem_limit_bytes=7 * MIB),
        cost_estimate=SMALL,
        name="rest",
    )(*near(*gs[0], gate_grad, up_grad, place, gate, up))
    return first, rest


def moved(value, by):
    count = lax.axis_size("expert")
    return lax.ppermute(value, "expert", [(i, (i + by) % count) for i in range(count)])


def swapped(value):
    return lax.ppermute(value, "expert", [(i, i ^ 1) for i in range(lax.axis_size("expert"))])


def moved_back(value, by):
    sections, count = lax.axis_size("section"), lax.axis_size("expert")
    pairs = [
        (s * count + i, ((s - 1) % sections) * count + (i + by) % count)
        for s in range(sections)
        for i in range(count)
    ]
    return lax.ppermute(value, ("section", "expert"), pairs)


def gathered_near(value):
    count = lax.axis_size("expert")
    if count != 4:
        return [value] + [moved(value, k) for k in range(1, count)]
    return [value, moved(value, 1), None, moved(value, -1)]


def gathered_far(who, blocks, done):
    if blocks[2] is not None:
        return blocks, None
    value, left, _, right = blocks
    passed = chosen(who, done, left, right)
    return [value, left, swapped(passed), right], passed


def joined_parts(who, parts, beside):
    if lax.axis_size("expert") != 4:
        return [(parts[k], -k) for k in range(1, len(parts))]
    _, left, far, right = parts
    to_left, to_right = joined(who, swapped(far), left, right, beside)
    return [(to_left, -1), (to_right, 1)]


def sum_kernel(count, *refs):
    total = refs[0][...].astype(F32)
    for ref in refs[1:count]:
        total = total + ref[...].astype(F32)
    refs[-1][...] = total.astype(BF16)


def write_kernel(count, start, *refs):
    out_ref, total_ref, sem = refs[-3:]
    sum_kernel(count, *refs[:count], total_ref)
    copy = pltpu.make_async_copy(total_ref, out_ref.at[:, start : start + total_ref.shape[1]], sem)
    copy.start()
    copy.wait()


def written(own, sent, start, width, result):
    terms = [own] + [moved(part, by) for part, by in sent]
    anywhere = pl.BlockSpec(memory_space=pl.ANY)
    return pl.pallas_call(
        functools.partial(write_kernel, len(terms), start),
        in_specs=[VMEM] * len(terms) + [anywhere] * len(result),
        out_specs=anywhere,
        out_shape=jax.ShapeDtypeStruct((own.shape[0], width), BF16),
        scratch_shapes=[pltpu.VMEM(own.shape, BF16), pltpu.SemaphoreType.DMA],
        input_output_aliases={len(terms): 0} if result else {},
        compiler_params=pltpu.CompilerParams(vmem_limit_bytes=2 * MIB),
        cost_estimate=SMALL,
        name="write",
    )(*near(*terms), *result)


def scattered(own, sent, last, after):
    move = moved if last else moved_back
    terms = [own] + [move(part, by) for part, by in sent]
    return pl.pallas_call(
        functools.partial(sum_kernel, len(terms)),
        in_specs=[VMEM] * (len(terms) + len(after)),
        out_specs=VMEM,
        out_shape=pltpu.VMEM(own.shape, BF16),
        compiler_params=pltpu.CompilerParams(vmem_limit_bytes=2 * MIB),
        cost_estimate=SMALL,
        name="sum",
    )(*near(*terms, *after))


def shards(grad_out, saved_inputs, routes, gate_weights, w_gate, w_up, w_down):
    gate, up, down = w_gate[0], w_up[0], w_down[0]
    local = gate.shape[0]
    tokens = grad_out.shape[1]
    steps = routes.shape[1]
    ringed = lax.axis_size("expert") == 4
    place = lax.axis_index("expert").astype(jnp.int32)
    who = ((place * local).reshape(1), (place % 2).reshape(1))
    first, grad = first_blocks(
        saved_inputs[0], grad_out[0], routes[0].transpose(0, 2, 1), gate_weights[0].transpose(0, 2, 1)
    )
    xs = gathered_near(first)
    gs = gathered_near(grad)
    *back, done = turned(who, first, gate, up, down)
    xs, passed = gathered_far(who, xs, done)
    metas = xs
    back[2], done = turned_into(back[2], passed if ringed else first, down)
    gs, passed = gathered_far(who, gs, done)
    gs = [[g] for g in gs]
    for step in range(steps):
        last = step + 1 == steps
        *factors, done = forward(step, who, tokens, xs, metas, back[0], back[1])
        if step:
            gs = [list(block) for block in zip(*[gathered_far(who, g, done)[0] for g in gs])]
        beside = ()
        if not last:
            following = held(saved_inputs[0], step + 1, passed) if ringed else saved_inputs[0, step + 1]
            xs = gathered_near(following)
            beside = xs[1::2] if ringed else ()
        halves = backward(CUTS[last], F32 if last else BF16, gs, *factors, *back)
        owns = [parts[0] if last else moved_back(parts[0], 0) for parts in halves]
        sent = []
        for own, parts in zip(owns, halves):
            sent.append(joined_parts(who, parts, (*beside, own)))
        if last:
            result, start = (), 0
            for own, pairs in zip(owns, sent):
                result = (written(own, pairs, start, grad_out.shape[2], result),)
                start += own.shape[1]
            return result[0][None]
        grads = []
        for own, pairs in zip(owns, sent):
            grads.append(scattered(own, pairs, last, grads))
        if not last:
            xs, _ = gathered_far(who, xs, done)
            gs = [gathered_near(grad) for grad in grads]


def solution(mesh):
    placed = (
        P("section", "expert", None),
        P("section", None, "expert", None),
        P("section", None, "expert", None),
        P("section", None, "expert", None),
        P("section", "expert", None, None),
        P("section", "expert", None, None),
        P("section", "expert", None, None),
    )
    return jax.shard_map(
        shards, mesh=mesh, in_specs=placed, out_specs=P("section", "expert", None), check_vma=False
    )
```

```python
import functools

import jax
import jax.numpy as jnp
from jax import lax
from jax.experimental import pallas as pl
from jax.experimental.pallas import tpu as pltpu
from jax.sharding import PartitionSpec as P

MOST = 40
PAIR = 2 * MOST
CUTS = (512, 512)
F32 = jnp.float32
BF16 = jnp.bfloat16


def dot(a, b, dims):
    return lax.dot_general(a, b, (dims, ((), ())), preferred_element_type=F32)


def expanded(local):
    slot = lax.broadcasted_iota(jnp.int32, (local, local * PAIR), 1)
    first = lax.broadcasted_iota(jnp.int32, (local, local * PAIR), 0) * PAIR
    return jnp.where((slot >= first) & (slot < first + PAIR), 1.0, 0.0).astype(BF16)


def forward_kernel(sources, local, tokens, step, base_ref, *refs):
    x_refs, refs = refs[:sources], refs[sources:]
    if step:
        meta_refs, refs = refs[:sources], refs[sources:]
    else:
        meta_refs = x_refs
    gate_ref, up_ref, a_ref, b_ref, pick_ref, place_ref, done_ref, rows_ref, weight_ref = refs
    count = a_ref.shape[0]
    top = x_refs[0].shape[1] // tokens

    mine = lax.broadcasted_iota(jnp.int32, (local, tokens), 0).astype(F32) + base_ref[0].astype(F32)
    before = (
        lax.broadcasted_iota(jnp.int32, (tokens, tokens), 0)
        < lax.broadcasted_iota(jnp.int32, (tokens, tokens), 1)
    )
    before = jnp.where(before, 1.0, 0.0).astype(BF16)
    table = expanded(local)
    for pair in range(sources // 2):
        targets, weights = [], []
        for half in range(2):
            meta = meta_refs[2 * pair + half][tokens:, :].astype(F32)[4 * step : 4 * step + 4]
            weights_of = meta[1:2] + meta[2:3] + meta[3:4]
            named = jnp.zeros((local, tokens), F32)
            weight = jnp.zeros((local, tokens), F32)
            for k in range(top):
                lanes = slice(k * tokens, (k + 1) * tokens)
                same = meta[0:1, lanes] == mine
                named = jnp.where(same, 1.0, named)
                weight = jnp.where(same, weights_of[:, lanes], weight)
            position = dot(named.astype(BF16), before, ((1,), (0,)))
            targets.append(jnp.where(named > 0.5, position + half * MOST, -1.0))
            weights.append(weight)
        target = jnp.concatenate(targets, axis=1).astype(BF16)
        weight = jnp.concatenate(weights, axis=1)
        spread = dot(table, target, ((0,), (0,)))
        slot = lax.broadcasted_iota(jnp.int32, spread.shape, 0) % PAIR
        picked = spread == slot.astype(F32)
        pick_ref[pair] = jnp.where(picked, 1.0, 0.0).astype(BF16)
        spread_t = dot(target, table, ((0,), (0,)))
        slot_t = lax.broadcasted_iota(jnp.int32, spread_t.shape, 1) % PAIR
        place_ref[pair] = jnp.where(spread_t == slot_t.astype(F32), 1.0, 0.0).astype(BF16)
        for e in range(local):
            block = jnp.where(picked[e * PAIR : (e + 1) * PAIR], weight[e : e + 1], 0.0)
            weight_ref[e, pair * PAIR : (pair + 1) * PAIR, :] = jnp.sum(block, axis=1, keepdims=True)
    pick_rows(x_refs, tokens, pick_ref, rows_ref)
    write_factors(0, count, rows_ref, weight_ref, gate_ref, up_ref, a_ref, b_ref)
    done_ref[...] = jnp.zeros_like(done_ref)


def write_factors(first, count, rows_ref, weight_ref, gate_ref, up_ref, a_ref, b_ref):
    for e in range(first, first + count):
        rows = rows_ref[e]
        gate = dot(rows, gate_ref[e], ((1,), (1,)))
        up = dot(rows, up_ref[e], ((1,), (1,)))
        sig = 1.0 / (1.0 + jnp.exp(-gate))
        scaled = sig * weight_ref[e]
        a_ref[e - first] = up * scaled * (1.0 + gate * (1.0 - sig))
        b_ref[e - first] = gate * scaled


def further_kernel(first, rows_ref, weight_ref, gate_ref, up_ref, after_ref, a_ref, b_ref):
    write_factors(first, a_ref.shape[0], rows_ref, weight_ref, gate_ref, up_ref, a_ref, b_ref)


def pick_rows(source_refs, tokens, pick_ref, rows_ref):
    local, width = rows_ref.shape[0], rows_ref.shape[2]
    for pair in range(len(source_refs) // 2):
        source = jnp.concatenate([ref[:tokens] for ref in source_refs[2 * pair : 2 * pair + 2]], axis=0)
        for n in range(0, width, 256):
            stop = min(n + 256, width)
            rows = dot(pick_ref[pair], source[:, n:stop], ((1,), (0,))).astype(BF16)
            rows_ref[:, pair * PAIR : (pair + 1) * PAIR, n:stop] = rows.reshape(local, PAIR, stop - n)


def pick_pieces(sources, pieces, piece_refs, pick_ref, rows_ref):
    start = 0
    for piece in range(pieces):
        refs = [piece_refs[k * pieces + piece] for k in range(sources)]
        tokens, width = refs[0].shape
        pick_rows(refs, tokens, pick_ref, rows_ref.at[:, :, start : start + width])
        start += width


def columns_of(refs, start, stop):
    parts, first = [], 0
    for ref in refs:
        last = first + ref.shape[1]
        if first < stop and start < last:
            parts.append(ref[:, max(start - first, 0) : min(stop, last) - first])
        first = last
    return jnp.concatenate(parts, axis=1)


def row_piece(kept_refs, gate_grad_ref, up_grad_ref, place_ref, gate_ref, up_ref, out_refs, back_ref, columns):
    local = gate_ref.shape[0]
    pairs, double = place_ref.shape[0], place_ref.shape[1]
    tokens = double // 2
    for e in range(local):
        row = dot(gate_grad_ref[e], gate_ref[e, :, columns], ((1,), (0,)))
        row = (row + dot(up_grad_ref[e], up_ref[e, :, columns], ((1,), (0,)))).astype(BF16)
        for pair in range(pairs):
            back_ref[pair, e] = row[pair * PAIR : (pair + 1) * PAIR]
    width = columns.stop - columns.start
    for pair in range(pairs):
        for n in range(0, width, 256):
            stop = min(n + 256, width)
            rows = back_ref[pair, :, :, n:stop].reshape(local * PAIR, stop - n)
            total = dot(place_ref[pair], rows, ((1,), (0,)))
            for half in range(2):
                out = out_refs[2 * pair + half]
                part = total[half * tokens : (half + 1) * tokens]
                if pair == 0 and half == 0:
                    part = part + columns_of(kept_refs, columns.start + n, columns.start + stop).astype(F32)
                out[:, n:stop] = part.astype(out.dtype)


def backward_kernel(sources, pieces, blocks, columns, *refs):
    g_refs, refs = refs[: sources * pieces], refs[sources * pieces :]
    a_refs, b_refs, refs = refs[:blocks], refs[blocks : 2 * blocks], refs[2 * blocks :]
    pick_ref, place_ref, gate_ref, up_ref, down_ref = refs[:5]
    out_refs, refs = refs[5 : 5 + sources], refs[5 + sources :]
    gate_grad_ref, up_grad_ref, rows_ref, back_ref = refs
    pick_pieces(sources, pieces, g_refs, pick_ref, rows_ref)
    for e in range(rows_ref.shape[0]):
        hidden = dot(rows_ref[e], down_ref[e], ((1,), (0,)))
        block, place = divmod(e, rows_ref.shape[0] // blocks)
        gate_grad_ref[e] = (hidden * a_refs[block][place]).astype(BF16)
        up_grad_ref[e] = (hidden * b_refs[block][place]).astype(BF16)
    row_piece(g_refs[:pieces], gate_grad_ref, up_grad_ref, place_ref, gate_ref, up_ref, out_refs, back_ref, columns)


def rest_kernel(sources, pieces, columns, *refs):
    kept_refs, refs = refs[:pieces], refs[pieces:]
    gate_grad_ref, up_grad_ref, place_ref, gate_ref, up_ref, *refs = refs
    row_piece(
        kept_refs, gate_grad_ref, up_grad_ref, place_ref, gate_ref, up_ref, refs[:sources], refs[sources], columns
    )


def hold_kernel(index, value_ref, *refs):
    refs[-1][...] = value_ref[index]


def turn_kernel(count, *refs):
    e = pl.program_id(0)
    refs = refs[3:]
    for from_ref, to_ref in zip(refs[:count], refs[count:]):
        to_ref[e] = from_ref[0].T
    refs[-1][...] = jnp.zeros_like(refs[-1])


def turn_into_kernel(from_ref, after_ref, held_ref, to_ref, done_ref):
    to_ref[pl.program_id(0)] = from_ref[0].T
    done_ref[...] = jnp.zeros_like(done_ref)


def first_kernel(saved_ref, grad_ref, routes_from, weights_from, out_ref, grad_out_ref, routes_ref, weights_ref, sems):
    tokens = saved_ref.shape[1]
    copies = [
        pltpu.make_async_copy(routes_from, routes_ref, sems.at[0]),
        pltpu.make_async_copy(weights_from, weights_ref, sems.at[1]),
        pltpu.make_async_copy(saved_ref.at[0], out_ref.at[:tokens], sems.at[2]),
        pltpu.make_async_copy(grad_ref, grad_out_ref, sems.at[3]),
    ]
    for copy in copies:
        copy.start()
    copies[0].wait()
    copies[1].wait()
    rows = []
    for step in range(routes_ref.shape[0]):
        weight = weights_ref[step]
        high = weight.astype(BF16).astype(F32)
        middle = (weight - high).astype(BF16).astype(F32)
        for part in (routes_ref[step].astype(F32), high, middle, weight - high - middle):
            rows.append(jnp.concatenate([part[k : k + 1] for k in range(part.shape[0])], axis=1))
    out_ref[tokens:] = jnp.concatenate(rows, axis=0).astype(BF16)
    for copy in copies[2:]:
        copy.wait()


VMEM = pl.BlockSpec(memory_space=pltpu.VMEM)
MIB = 1024 * 1024
SMALL = pl.CostEstimate(flops=0, bytes_accessed=1024, transcendentals=0)
DONE = pltpu.VMEM((8, 128), F32)


def near(*values):
    return [pltpu.with_memory_space_constraint(v, pltpu.VMEM) for v in values]


def one(shape):
    return pl.BlockSpec((1,) + shape[1:], lambda e: (e,) + (0,) * (len(shape) - 1))


def turned(who, after, *weights):
    local = weights[0].shape[0]
    shapes = [(local, w.shape[2], w.shape[1]) for w in weights]
    return pl.pallas_call(
        functools.partial(turn_kernel, len(weights) - 1),
        grid=(local,),
        in_specs=[pl.BlockSpec(memory_space=pltpu.SMEM)] * 2 + [VMEM] + [one(w.shape) for w in weights[:-1]],
        out_specs=(VMEM,) * (len(weights) + 1),
        out_shape=(*[pltpu.VMEM(shape, BF16) for shape in shapes], DONE),
        compiler_params=pltpu.CompilerParams(vmem_limit_bytes=10 * MIB),
        cost_estimate=SMALL,
        name="turn",
    )(*who, *near(after), *[pltpu.with_memory_space_constraint(w, pltpu.HBM) for w in weights[:-1]])


def turned_into(place, after, weight):
    return pl.pallas_call(
        turn_into_kernel,
        grid=(weight.shape[0],),
        in_specs=[one(weight.shape), VMEM, VMEM],
        out_specs=(VMEM, VMEM),
        out_shape=(pltpu.VMEM(place.shape, BF16), DONE),
        input_output_aliases={2: 0},
        compiler_params=pltpu.CompilerParams(vmem_limit_bytes=6 * MIB),
        cost_estimate=SMALL,
        name="turn_into",
    )(pltpu.with_memory_space_constraint(weight, pltpu.HBM), *near(after, place))


def first_blocks(saved, grad, routes, weights):
    steps, tokens, width = saved.shape
    return pl.pallas_call(
        first_kernel,
        in_specs=[pl.BlockSpec(memory_space=pl.ANY)] * 4,
        out_specs=(VMEM,) * 2,
        out_shape=(pltpu.VMEM((tokens + 4 * steps, width), BF16), pltpu.VMEM(grad.shape, BF16)),
        scratch_shapes=[
            pltpu.VMEM(routes.shape, routes.dtype),
            pltpu.VMEM(weights.shape, weights.dtype),
            pltpu.SemaphoreType.DMA((4,)),
        ],
        compiler_params=pltpu.CompilerParams(vmem_limit_bytes=2 * MIB),
        cost_estimate=SMALL,
        name="first",
    )(*[pltpu.with_memory_space_constraint(v, pltpu.HBM) for v in (saved, grad, routes, weights)])


def choose_kernel(odd_ref, done_ref, left_ref, right_ref, out_ref):
    @pl.when(odd_ref[0] == 1)
    def _():
        out_ref[...] = right_ref[...]

    @pl.when(odd_ref[0] == 0)
    def _():
        out_ref[...] = left_ref[...]


def chosen(who, done, left, right):
    done = left if done is who[1] else done
    return pl.pallas_call(
        choose_kernel,
        in_specs=[pl.BlockSpec(memory_space=pltpu.SMEM)] + [VMEM] * 3,
        out_specs=VMEM,
        out_shape=pltpu.VMEM(left.shape, left.dtype),
        compiler_params=pltpu.CompilerParams(vmem_limit_bytes=2 * MIB),
        cost_estimate=SMALL,
        name="choose",
    )(who[1], *near(done, left, right))


def join_kernel(odd_ref, far_ref, left_ref, right_ref, *refs):
    to_left_ref, to_right_ref = refs[-2:]
    far = far_ref[...].astype(F32)

    @pl.when(odd_ref[0] == 1)
    def _():
        to_left_ref[...] = left_ref[...]
        to_right_ref[...] = (right_ref[...].astype(F32) + far).astype(BF16)

    @pl.when(odd_ref[0] == 0)
    def _():
        to_left_ref[...] = (left_ref[...].astype(F32) + far).astype(BF16)
        to_right_ref[...] = right_ref[...]


def joined(who, far, left, right, beside):
    return pl.pallas_call(
        join_kernel,
        in_specs=[pl.BlockSpec(memory_space=pltpu.SMEM)] + [VMEM] * (3 + len(beside)),
        out_specs=(VMEM,) * 2,
        out_shape=(pltpu.VMEM(left.shape, left.dtype),) * 2,
        compiler_params=pltpu.CompilerParams(vmem_limit_bytes=2 * MIB),
        cost_estimate=SMALL,
        name="join",
    )(who[1], *near(far, left, right, *beside))


def held(value, index, *after):
    return pl.pallas_call(
        functools.partial(hold_kernel, index),
        in_specs=[VMEM] * (1 + len(after)),
        out_specs=VMEM,
        out_shape=pltpu.VMEM(value.shape[1:], value.dtype),
        compiler_params=pltpu.CompilerParams(vmem_limit_bytes=2 * MIB),
        cost_estimate=SMALL,
        name="hold",
    )(*near(value, *after))


def forward(step, who, tokens, xs, metas, gate, up, count):
    sources, local = len(xs), gate.shape[0]
    width = xs[0].shape[1]
    hidden = gate.shape[1]
    rows = sources * MOST
    arrays = (*xs, *metas, gate, up) if step else (*xs, gate, up)
    kept = (pltpu.VMEM((local, rows, width), BF16), pltpu.VMEM((local, rows, 1), F32))
    shared = kept if count < local else ()
    a, b, pick, place, done, *others = pl.pallas_call(
        functools.partial(forward_kernel, sources, local, tokens, step),
        in_specs=[pl.BlockSpec(memory_space=pltpu.SMEM)] + [VMEM] * len(arrays),
        out_specs=(VMEM,) * (5 + len(shared)),
        out_shape=(
            pltpu.VMEM((count, rows, hidden), F32),
            pltpu.VMEM((count, rows, hidden), F32),
            pltpu.VMEM((sources // 2, local * PAIR, 2 * tokens), BF16),
            pltpu.VMEM((sources // 2, 2 * tokens, local * PAIR), BF16),
            DONE,
            *shared,
        ),
        scratch_shapes=[] if shared else list(kept),
        compiler_params=pltpu.CompilerParams(vmem_limit_bytes=9 * MIB),
        cost_estimate=SMALL,
        name="forward",
    )(who[0], *near(*arrays))
    return [a], [b], (pick, place), (*others, gate, up), done


def further(count, picked, weight, gate, up, after):
    local, rows = picked.shape[:2]
    shape = (local - count, rows, gate.shape[1])
    return pl.pallas_call(
        functools.partial(further_kernel, count),
        in_specs=[VMEM] * 5,
        out_specs=(VMEM,) * 2,
        out_shape=(pltpu.VMEM(shape, F32),) * 2,
        compiler_params=pltpu.CompilerParams(vmem_limit_bytes=6 * MIB),
        cost_estimate=SMALL,
        name="further",
    )(*near(picked, weight, gate, up, after))


def backward(cut, kept_type, gs, factors_a, factors_b, pick, place, gate, up, down):
    sources, pieces, local = len(gs), len(gs[0]), gate.shape[0]
    tokens = gs[0][0].shape[0]
    hidden, width = gate.shape[1:]
    rows = sources * MOST
    types = [kept_type] + [BF16] * (sources - 1)
    outs = [tuple(pltpu.VMEM((tokens, w), t) for t in types) for w in (cut, width - cut)]
    factor = pltpu.VMEM((local, rows, hidden), BF16)
    backs = [pltpu.VMEM((sources // 2, local, PAIR, w), BF16) for w in (cut, width - cut)]
    *first, gate_grad, up_grad = pl.pallas_call(
        functools.partial(backward_kernel, sources, pieces, len(factors_a), slice(0, cut)),
        in_specs=[VMEM] * (sources * pieces + 2 * len(factors_a) + 5),
        out_specs=(VMEM,) * (sources + 2),
        out_shape=outs[0] + (factor, factor),
        scratch_shapes=[pltpu.VMEM((local, rows, width), BF16), backs[0]],
        compiler_params=pltpu.CompilerParams(vmem_limit_bytes=11 * MIB),
        cost_estimate=SMALL,
        name="backward",
    )(*near(*[g for block in gs for g in block], *factors_a, *factors_b, pick, place, gate, up, down))
    rest = pl.pallas_call(
        functools.partial(rest_kernel, sources, pieces, slice(cut, width)),
        in_specs=[VMEM] * (pieces + 5),
        out_specs=(VMEM,) * sources,
        out_shape=outs[1],
        scratch_shapes=[backs[1]],
        compiler_params=pltpu.CompilerParams(vmem_limit_bytes=7 * MIB),
        cost_estimate=SMALL,
        name="rest",
    )(*near(*gs[0], gate_grad, up_grad, place, gate, up))
    return first, rest


def moved(value, by):
    count = lax.axis_size("expert")
    return lax.ppermute(value, "expert", [(i, (i + by) % count) for i in range(count)])


def swapped(value):
    return lax.ppermute(value, "expert", [(i, i ^ 1) for i in range(lax.axis_size("expert"))])


def moved_back(value, by):
    sections, count = lax.axis_size("section"), lax.axis_size("expert")
    pairs = [
        (s * count + i, ((s - 1) % sections) * count + (i + by) % count)
        for s in range(sections)
        for i in range(count)
    ]
    return lax.ppermute(value, ("section", "expert"), pairs)


def gathered_near(value):
    count = lax.axis_size("expert")
    if count != 4:
        return [value] + [moved(value, k) for k in range(1, count)]
    return [value, moved(value, 1), None, moved(value, -1)]


def gathered_far(who, blocks, done):
    if blocks[2] is not None:
        return blocks, None
    value, left, _, right = blocks
    passed = chosen(who, done, left, right)
    return [value, left, swapped(passed), right], passed


def joined_parts(who, parts, beside):
    if lax.axis_size("expert") != 4:
        return [(parts[k], -k) for k in range(1, len(parts))]
    _, left, far, right = parts
    to_left, to_right = joined(who, swapped(far), left, right, beside)
    return [(to_left, -1), (to_right, 1)]


def sum_kernel(count, *refs):
    total = refs[0][...].astype(F32)
    for ref in refs[1:count]:
        total = total + ref[...].astype(F32)
    refs[-1][...] = total.astype(BF16)


def write_kernel(count, start, *refs):
    out_ref, total_ref, sem = refs[-3:]
    sum_kernel(count, *refs[:count], total_ref)
    copy = pltpu.make_async_copy(total_ref, out_ref.at[:, start : start + total_ref.shape[1]], sem)
    copy.start()
    copy.wait()


def written(own, sent, start, width, result):
    terms = [own] + [moved(part, by) for part, by in sent]
    anywhere = pl.BlockSpec(memory_space=pl.ANY)
    return pl.pallas_call(
        functools.partial(write_kernel, len(terms), start),
        in_specs=[VMEM] * len(terms) + [anywhere] * len(result),
        out_specs=anywhere,
        out_shape=jax.ShapeDtypeStruct((own.shape[0], width), BF16),
        scratch_shapes=[pltpu.VMEM(own.shape, BF16), pltpu.SemaphoreType.DMA],
        input_output_aliases={len(terms): 0} if result else {},
        compiler_params=pltpu.CompilerParams(vmem_limit_bytes=2 * MIB),
        cost_estimate=SMALL,
        name="write",
    )(*near(*terms), *result)


def scattered(own, sent, last, after):
    move = moved if last else moved_back
    terms = [own] + [move(part, by) for part, by in sent]
    return pl.pallas_call(
        functools.partial(sum_kernel, len(terms)),
        in_specs=[VMEM] * (len(terms) + len(after)),
        out_specs=VMEM,
        out_shape=pltpu.VMEM(own.shape, BF16),
        compiler_params=pltpu.CompilerParams(vmem_limit_bytes=2 * MIB),
        cost_estimate=SMALL,
        name="sum",
    )(*near(*terms, *after))


def shards(grad_out, saved_inputs, routes, gate_weights, w_gate, w_up, w_down):
    gate, up, down = w_gate[0], w_up[0], w_down[0]
    local = gate.shape[0]
    tokens = grad_out.shape[1]
    steps = routes.shape[1]
    ringed = lax.axis_size("expert") == 4
    place = lax.axis_index("expert").astype(jnp.int32)
    who = ((place * local).reshape(1), (place % 2).reshape(1))
    first, grad = first_blocks(
        saved_inputs[0], grad_out[0], routes[0].transpose(0, 2, 1), gate_weights[0].transpose(0, 2, 1)
    )
    xs = gathered_near(first)
    gs = gathered_near(grad)
    *back, done = turned(who, first, gate, up, down)
    xs, passed = gathered_far(who, xs, done)
    metas = xs
    back[2], done = turned_into(back[2], passed if ringed else first, down)
    gs, passed = gathered_far(who, gs, done)
    gs = [[g] for g in gs]
    for step in range(steps):
        last = step + 1 == steps
        count = local // 2 if step and ringed else local
        a, b, tables, others, done = forward(step, who, tokens, xs, metas, back[0], back[1], count)
        if step:
            pieces = [gathered_far(who, g, done) for g in gs]
            gs = [list(block) for block in zip(*[piece for piece, _ in pieces])]
        if count < local:
            more_a, more_b = further(count, *others, pieces[-1][1])
            a, b = a + [more_a], b + [more_b]
        beside = ()
        if not last:
            following = held(saved_inputs[0], step + 1, passed) if ringed else saved_inputs[0, step + 1]
            xs = gathered_near(following)
            beside = xs[1::2] if ringed else ()
        halves = backward(CUTS[last], F32 if last else BF16, gs, a, b, *tables, *back)
        owns = [parts[0] if last else moved_back(parts[0], 0) for parts in halves]
        sent = []
        for own, parts in zip(owns, halves):
            sent.append(joined_parts(who, parts, (*beside, own)))
        if last:
            result, start = (), 0
            for own, pairs in zip(owns, sent):
                result = (written(own, pairs, start, grad_out.shape[2], result),)
                start += own.shape[1]
            return result[0][None]
        grads = []
        for own, pairs in zip(owns, sent):
            grads.append(scattered(own, pairs, last, grads))
        if not last:
            xs, _ = gathered_far(who, xs, done)
            gs = [gathered_near(grad) for grad in grads]


def solution(mesh):
    placed = (
        P("section", "expert", None),
        P("section", None, "expert", None),
        P("section", None, "expert", None),
        P("section", None, "expert", None),
        P("section", "expert", None, None),
        P("section", "expert", None, None),
        P("section", "expert", None, None),
    )
    return jax.shard_map(
        shards, mesh=mesh, in_specs=placed, out_specs=P("section", "expert", None), check_vma=False
    )
```
